32 devices in a mesh: row: 8 (over y, x, core), col: 4 (over z).
Axes of the slice: x: 2, y: 2, z: 4, core: 2. Of those that a mesh axis runs over, the one named last changes fastest.
Arguments:
- matrix: float32 [5120, 8192], P('row', 'col'), may hold values from -100 to 100
- pivots: int32 [256], replicated, may hold values from 0 to 8191, as said below
- sketch: float32 [264, 8192], P(None, ('col', 'row')), may hold values from -6 to 6
Outputs:
- upper_rows: float32 [256, 8192], P(None, ('col', 'row'))
- trailing: float32 [5120, 8192], P('row', 'col')
- new_sketch: float32 [264, 8192], P(None, ('col', 'row'))
The draws below stay inside these ranges and needn't reach their ends.
Inputs may be any that keep to these rules, and one draw needn't show every extreme that they name: `pivots`: 256 distinct column indices.
All inputs are finite; a program needn't handle non-finite values.
Results may differ from the reference program's by a relative error of at most 0.0003.
Values sent between devices are 32-bit elements; how exact they have to be, the bound alone decides.
A program may use at most 128 MiB of HBM per device.

```python
import math
import jax
import jax.numpy as jnp
from jax import lax

BLOCK_COLUMNS = 256
SK = 264
COLUMNS_PER_SHARD = 2048
ROWS = 5120
MATRIX_COLUMNS = 8192


def draw_matrix(key, part):
    keys = jax.random.split(jax.random.fold_in(key, 11), 6)
    along = jnp.arange(ROWS, dtype=jnp.float32) / (ROWS - 1)
    shared = jnp.clip(jax.random.normal(keys[3], (ROWS, 2), jnp.float32), -3.0, 3.0)
    noise = jnp.clip(jax.random.normal(keys[0], (ROWS, MATRIX_COLUMNS), jnp.float32), -5.0, 5.0)
    leading = jax.random.uniform(keys[4], (1, MATRIX_COLUMNS), jnp.float32, 0.1, 0.2)
    row_spread = 0.5
    second = jax.random.uniform(keys[5], (1, MATRIX_COLUMNS), jnp.float32, -0.1, 0.1)
    values = (noise + shared[:, 0:1] * leading + shared[:, 1:2] * second) / math.sqrt(ROWS)
    rough_rows = jax.random.uniform(keys[1], (ROWS,), jnp.float32, -row_spread, row_spread)
    rows_scale = 3.0 ** (along - 0.5) * 10.0 ** rough_rows
    col_scale = 10.0 ** jax.random.uniform(keys[2], (MATRIX_COLUMNS,), jnp.float32, -0.3, 0.3)
    return (values * rows_scale[:, None] * col_scale[None, :]).astype(jnp.float32)


def draw_pivots(key, part):
    keys = jax.random.split(jax.random.fold_in(key, 23), 2)
    column_position = jnp.arange(MATRIX_COLUMNS, dtype=jnp.int32)
    ranking_levels = jax.random.randint(keys[0], (MATRIX_COLUMNS // COLUMNS_PER_SHARD,), 0, 3).astype(jnp.int32)
    starting_column = jax.random.permutation(keys[1], MATRIX_COLUMNS).astype(jnp.int32)
    priority_boost = ranking_levels[column_position // COLUMNS_PER_SHARD] * (MATRIX_COLUMNS // 4) + (column_position < BLOCK_COLUMNS).astype(jnp.int32) * (MATRIX_COLUMNS // 4)
    ends_boost = ((column_position == 0) | (column_position == MATRIX_COLUMNS - 1)).astype(jnp.int32) * (2 * MATRIX_COLUMNS)
    column_scores = (starting_column + priority_boost + ends_boost) * MATRIX_COLUMNS + column_position
    ranked, chosen = lax.top_k(column_scores, BLOCK_COLUMNS)
    return chosen.astype(jnp.int32)


def block_scale(stream_key, extent, pieces, smallest, largest):
    level, own = 1.0, jax.random.fold_in(stream_key, 6)
    for position, blocks in pieces:
        steps = jnp.exp(jax.random.uniform(jax.random.fold_in(own, position), (blocks,), jnp.float32, smallest / len(pieces), largest / len(pieces)))
        level = level * jnp.repeat(steps, extent[position] // blocks).reshape([-1 if axis == position else 1 for axis in range(len(extent))])
    return level


def centred(stream_key, shape, deviation, reach, shards=(), held_as=jnp.bfloat16):
    gain = block_scale(stream_key, shape, shards, -0.22, 0.18) if shards else 1.0
    result = jax.random.normal(stream_key, shape, jnp.float32) * deviation * gain
    return jnp.minimum(jnp.maximum(result, -reach), reach).astype(held_as)


def setup_inputs(seed: int = 0) -> dict:
    splits = jax.random.split(jax.random.key(seed), 4)
    matrix = draw_matrix(jax.random.fold_in(splits[3], 71), 0)
    pivots = draw_pivots(jax.random.fold_in(splits[3], 71), 0)
    sketch = centred(splits[2], (SK, MATRIX_COLUMNS), 1.0, 6.0, ((1, 32),), jnp.float32)
    return dict(matrix=matrix, pivots=pivots, sketch=sketch)


sentinel_value = 1 << 30
highest = lax.Precision.HIGHEST

def pairing(pivots, panel_cols):
    positions = jnp.arange(panel_cols, dtype=jnp.int32)
    present = jnp.any(pivots[None, :] == positions[:, None], axis=1)
    displaced = jnp.sort(jnp.where(present, sentinel_value, positions).astype(jnp.int32))
    vacated = jnp.sort(jnp.where(pivots >= panel_cols, pivots, sentinel_value).astype(jnp.int32))
    return (vacated, displaced)

def reference(matrix, pivots, sketch):
    vacated, displaced = pairing(pivots, BLOCK_COLUMNS)
    order = jnp.arange(MATRIX_COLUMNS, dtype=jnp.int32)
    order = order.at[vacated].set(displaced, mode='drop')
    order = order.at[:BLOCK_COLUMNS].set(pivots.astype(jnp.int32))
    permuted = jnp.take(matrix, order, axis=1)
    panel = permuted[:, :BLOCK_COLUMNS]
    basis, upper = jnp.linalg.qr(panel)
    signs = jnp.sign(jnp.diagonal(upper))
    basis = basis * signs[None, :]
    upper = upper * signs[:, None]
    upper_rows = jnp.dot(basis.T.astype(jnp.float32), permuted.astype(jnp.float32), precision=highest, preferred_element_type=jnp.float32)
    trailing = permuted - jnp.dot(basis.astype(jnp.float32), upper_rows.astype(jnp.float32), precision=highest, preferred_element_type=jnp.float32)
    moved = jnp.take(sketch, order, axis=1)
    solved = lax.linalg.triangular_solve(upper, upper_rows, left_side=True, lower=False)
    new_sketch = moved - jnp.dot(moved[:, :BLOCK_COLUMNS].astype(jnp.float32), solved.astype(jnp.float32), precision=highest, preferred_element_type=jnp.float32)
    return (upper_rows, trailing, new_sketch)
```

```python
import functools

import jax
import jax.numpy as jnp
from jax import lax
from jax.experimental import pallas as pl
from jax.experimental.pallas import tpu as pltpu
from jax.sharding import PartitionSpec as P

highest = lax.Precision.HIGHEST
f32 = jnp.float32
bf16 = jnp.bfloat16
MESH = pl.DeviceIdType.MESH
NN = (((1,), (0,)), ((), ()))
NT = (((1,), (1,)), ((), ()))
TN = (((0,), (0,)), ((), ()))


def dot(a, b, dims=NN, precision=None):
    return lax.dot_general(a, b, dims, precision=precision, preferred_element_type=f32)


def two(x):
    high = x.astype(bf16)
    return high, (x - high.astype(f32)).astype(bf16)


def three(x):
    high = x.astype(bf16)
    rest = x - high.astype(f32)
    mid = rest.astype(bf16)
    return high, mid, (rest - mid.astype(f32)).astype(bf16)


def dot3(a, b, dims=NN):
    (ah, al), (bh, bl) = a, b
    return dot(ah, bh, dims) + (dot(ah, bl, dims) + dot(al, bh, dims))


def pick3(parts, onehot):
    high, mid, low = parts
    return (dot(low, onehot) + dot(mid, onehot)) + dot(high, onehot)


def iota(shape, axis):
    return lax.broadcasted_iota(jnp.int32, shape, axis)


def cholesky_block(aug, linv, b, width):
    n = aug.shape[0]
    lo = b * width
    d = aug[lo : lo + width, lo : lo + width]
    v = jnp.where(iota((width, width), 0) == iota((width, width), 1), 1.0, 0.0).astype(f32)
    below = iota((width, 1), 0)
    lane = iota((1, width), 1)
    diag = jnp.ones((width, 1), f32)
    for i in range(width):
        pivot = d[i : i + 1, i : i + 1]
        diag = jnp.where(below == i, pivot, diag)
        if i < width - 1:
            m = jnp.where(below > i, d[:, i : i + 1] * (1.0 / pivot), 0.0)
            d = d - m * d[i : i + 1, :]
            v = v - m * v[i : i + 1, :]
    v = v * lax.rsqrt(diag)
    rows = dot(v, aug[lo : lo + width, :], precision=highest)
    linv[lo : lo + width, :] = rows[:, n:]
    if lo + width < n:
        down = dot(rows[:, :n], rows, TN, highest)
        aug[lo + width :, :] = aug[lo + width :, :] - down[lo + width :, :]


def kernel(
    nrow, ncol, chunks, width,
    x, piv_row, piv_col, partner,
    perm_hbm, w_out, summed, upper_out, solved_out,
    onehot, picked, moved_in, from_left, from_right, to_right, to_left,
    panel, perm, product, core_in, reduce_in, totals, gram, gram_in, gram_parts, aug, linv,
    zr_s, zr_r, zl_s, zl_r, g1, g2_s, g2_r, g3, c_s, c_r, r_s, r_r, a_s, a_r, f_s, f_r, out_sem,
):
    rows, columns = x.shape
    n = panel.shape[1]
    tiles = columns // n
    chips = nrow // 2
    share = columns // nrow
    me = lax.axis_index("row")
    z = lax.axis_index("col")
    core = lax.rem(me, 2)
    chip = me // 2
    mate = me + 1 - 2 * core

    def remote(src, dst, ss, rs, dev):
        return pltpu.make_async_remote_copy(
            src_ref=src, dst_ref=dst, send_sem=ss, recv_sem=rs, device_id=dev, device_id_type=MESH
        )

    def peer(d):
        return lax.rem(chip + d, chips) * 2 + core

    def origin(d):
        return lax.rem(chip + chips - d, chips)

    barrier = pltpu.get_barrier_semaphore()

    @pl.when(z > 0)
    def _():
        pl.semaphore_signal(barrier, inc=1, device_id={"col": z - 1}, device_id_type=MESH)

    @pl.when(z < ncol - 1)
    def _():
        pl.semaphore_signal(barrier, inc=1, device_id={"col": z + 1}, device_id_type=MESH)

    pl.semaphore_signal(barrier, inc=1, device_id={"row": mate}, device_id_type=MESH)
    for d in range(1, chips):
        pl.semaphore_signal(barrier, inc=1, device_id={"row": peer(d)}, device_id_type=MESH)

    offset = z * columns
    local = piv_row[...] - offset
    mine = (local >= 0) & (local < columns)
    before = local < 0

    @pl.loop(0, tiles)
    def _(t):
        at = pl.multiple_of(t * n, n)
        onehot[pl.ds(at, n), :] = jnp.where(iota((n, n), 0) + at == local, 1.0, 0.0).astype(bf16)

    former_hot = jnp.where(iota((n, n), 0) == partner[...], 1.0, 0.0).astype(bf16)
    size = rows // chunks

    @pl.loop(0, chunks)
    def _(c):
        at = pl.ds(pl.multiple_of(c * size, size), size)
        picked[at, :] = pick3(three(x[at, :]), onehot[...])

    @pl.when(z == 0)
    def _():
        @pl.loop(0, chunks)
        def _(c):
            at = pl.ds(pl.multiple_of(c * size, size), size)
            moved_in[at, :] = pick3(three(x[at, :n]), former_hot)

    pl.semaphore_wait(
        barrier, chips + jnp.where(z > 0, 1, 0) + jnp.where(z < ncol - 1, 1, 0)
    )

    def right(c):
        at = pl.ds(pl.multiple_of(c * size, size), size)
        return remote(to_right.at[at, :], from_left.at[at, :], zr_s.at[c], zr_r.at[c], {"col": z + 1})

    def left(c):
        at = pl.ds(pl.multiple_of(c * size, size), size)
        return remote(to_left.at[at, :], from_right.at[at, :], zl_s.at[c], zl_r.at[c], {"col": z - 1})

    @pl.loop(0, chunks + ncol - 1)
    def _(t):
        c = t - z

        @pl.when((c >= 0) & (c < chunks))
        def _():
            at = pl.ds(pl.multiple_of(c * size, size), size)

            @pl.when(z > 0)
            def _():
                right(c).wait_recv()
                moved_in[at, :] = from_left[at, :]

            @pl.when(z < ncol - 1)
            def _():
                to_right[at, :] = jnp.where(mine, picked[at, :], moved_in[at, :])
                right(c).start()

        e = t - (ncol - 1 - z)

        @pl.when((e >= 0) & (e < chunks))
        def _():
            at = pl.ds(pl.multiple_of(e * size, size), size)

            @pl.when(z < ncol - 1)
            def _():
                left(e).wait_recv()
                panel[at, :] = jnp.where(mine, picked[at, :], from_right[at, :])

            @pl.when(z == ncol - 1)
            def _():
                panel[at, :] = picked[at, :]

            @pl.when(z > 0)
            def _():
                to_left[at, :] = panel[at, :]
                left(e).start()

    panel[...] = jnp.where(before, moved_in[...], panel[...])

    half = n // 2
    columns_of = panel[...].T
    gram[...] = dot(columns_of, panel[...], precision=highest)
    first = remote(gram, gram_in, g1.at[0], g1.at[1], {"row": mate})
    first.start()

    left_parts = two(columns_of)
    former = three(moved_in[...])
    wanted = piv_col[...] - offset
    usable = piv_col[...] >= n

    def out_copy(t):
        at = pl.ds(pl.multiple_of(t * n, n), n)
        return pltpu.make_async_copy(perm.at[:, at], perm_hbm.at[:, at], out_sem.at[t])

    @pl.loop(0, tiles)
    def _(t):
        at = pl.multiple_of(t * n, n)
        place = (iota((n, n), 1) + at == wanted) & usable
        place = jnp.where(place, 1.0, 0.0)
        keep = 1.0 - jnp.sum(place, axis=0, keepdims=True)
        tile = x[:, pl.ds(at, n)] * keep + pick3(former, place.astype(bf16))
        tile = jnp.where((z == 0) & (t == 0), panel[...], tile)
        perm[:, pl.ds(at, n)] = tile
        out_copy(t).start()
        product[pl.ds(at, n), :] = dot3(left_parts, two(tile)).T

    def part(owner):
        return pl.ds(pl.multiple_of(owner * share, share), share)

    def to_mate(c):
        return remote(product.at[part(2 * c + 1 - core), :], core_in.at[c], c_s.at[c], c_r.at[c], {"row": mate})

    for c in range(chips):
        to_mate(c).start()

    first.wait()
    mine_rows = pl.ds(pl.multiple_of(core * half, half), half)
    other_rows = pl.ds(pl.multiple_of((1 - core) * half, half), half)
    gram_parts[0, :, :] = gram[mine_rows, :] + gram_in[mine_rows, :]

    def gram_to(d):
        return remote(gram_parts.at[0], gram_parts.at[d], g2_s.at[d], g2_r.at[d], {"row": peer(d)})

    for d in range(1, chips):
        gram_to(d).start()

    for c in range(chips):
        to_mate(c).wait()
        totals[c, :, :] = product[part(2 * c + core), :] + core_in[c, :, :]

    def reduce_to(d):
        return remote(totals.at[lax.rem(chip + d, chips)], reduce_in.at[d], r_s.at[d], r_r.at[d], {"row": peer(d)})

    for d in range(1, chips):
        reduce_to(d).start()

    for d in range(1, chips):
        gram_to(d).wait()
    gram_half = jnp.zeros((half, n), f32)
    for d in range(chips):
        gram_half = gram_half + gram_parts[lax.rem(chip + chips - d, chips), :, :]
    aug[mine_rows, :n] = gram_half
    last = remote(aug.at[mine_rows, :n], aug.at[mine_rows, :n], g3.at[0], g3.at[1], {"row": mate})
    last.start()
    aug[:, n:] = jnp.where(iota((n, n), 0) == iota((n, n), 1), 1.0, 0.0).astype(f32)
    last.wait_send()
    remote(aug.at[other_rows, :n], aug.at[other_rows, :n], g3.at[0], g3.at[1], {"row": mate}).wait_recv()

    def gather_to(d):
        return remote(summed.at[part(me), :], summed.at[part(me), :], a_s.at[d], a_r.at[d], {"row": peer(d)})

    def gathered(d):
        at = part(origin(d) * 2 + core)
        return remote(summed.at[at, :], summed.at[at, :], a_s.at[d], a_r.at[d], {"row": peer(d)})

    def forward(d):
        at = part(origin(d) * 2 + core)
        return remote(summed.at[at, :], summed.at[at, :], f_s.at[d], f_r.at[d], {"row": mate})

    def forwarded(d):
        at = part(origin(d) * 2 + 1 - core)
        return remote(summed.at[at, :], summed.at[at, :], f_s.at[d], f_r.at[d], {"row": mate})

    def finish_reduce():
        total = totals[chip, :, :]
        for d in range(1, chips):
            reduce_to(d).wait()
            total = total + reduce_in[d, :, :]
        summed[part(me), :] = total
        for d in range(1, chips):
            gather_to(d).start()
        forward(0).start()

    def finish_gather():
        for d in range(1, chips):
            gathered(d).wait_recv()
            forward(d).start()

    blocks = n // width
    for b in range(blocks):
        cholesky_block(aug, linv, b, width)
        if b == blocks // 2 - 1:
            finish_reduce()
    finish_gather()

    inverse = dot(linv[...], linv[...], TN, highest)
    w_out[...] = dot(panel[...], inverse, precision=highest)
    own = summed[part(me), :]
    upper_out[...] = dot(linv[...], own, NT, highest)
    solved_out[...] = dot(inverse, own, NT, highest)

    for d in range(chips):
        forwarded(d).wait_recv()
    for d in range(1, chips):
        gather_to(d).wait_send()
    for d in range(chips):
        forward(d).wait_send()

    @pl.loop(0, chunks)
    def _(c):
        @pl.when(z < ncol - 1)
        def _():
            right(c).wait_send()

        @pl.when(z > 0)
        def _():
            left(c).wait_send()

    @pl.loop(0, tiles)
    def _(t):
        out_copy(t).wait()


def project(perm, w, summed, out):
    out[...] = perm[...] - dot3(two(w[...]), two(summed[...]), NT)


def hot(condition):
    return jnp.where(condition, 1.0, 0.0).astype(f32)


def per_device(nrow, ncol, matrix, pivots, sketch):
    rows, columns = matrix.shape
    n = pivots.shape[0]
    pieces = sketch.shape[1]
    positions = jnp.arange(n, dtype=jnp.int32)
    absent = ~jnp.any(pivots[None, :] == positions[:, None], axis=1)
    place = jnp.sum((absent[None, :] & (positions[None, :] < positions[:, None])).astype(jnp.int32), axis=1)
    rank = jnp.sum(((pivots[None, :] >= n) & (pivots[None, :] < pivots[:, None])).astype(jnp.int32), axis=1)
    partner = jnp.sum(
        jnp.where(absent[None, :] & (place[None, :] == rank[:, None]), positions[None, :], 0), axis=1
    )

    start = (lax.axis_index("col") * nrow + lax.axis_index("row")) * pieces
    spots = start + jnp.arange(pieces, dtype=jnp.int32)
    both = jnp.concatenate([pivots, partner])
    picks = jnp.dot(sketch, hot(spots[:, None] == both[None, :]), precision=highest)
    fronts_former = lax.psum(picks, ("row", "col"))

    chunks = 10
    width = 32
    chips = nrow // 2
    share = columns // nrow
    vmem = pl.BlockSpec(memory_space=pltpu.VMEM)
    full = pltpu.VMEM((rows, n), f32)
    dma = pltpu.SemaphoreType.DMA
    perm, w, summed, upper, solved = pl.pallas_call(
        functools.partial(kernel, nrow, ncol, chunks, width),
        out_shape=[
            jax.ShapeDtypeStruct((rows, columns), f32),
            jax.ShapeDtypeStruct((rows, n), f32),
            jax.ShapeDtypeStruct((columns, n), f32),
            jax.ShapeDtypeStruct((n, share), f32),
            jax.ShapeDtypeStruct((n, share), f32),
        ],
        in_specs=[vmem] * 4,
        out_specs=[pl.BlockSpec(memory_space=pl.ANY)] + [vmem] * 4,
        scratch_shapes=[
            pltpu.VMEM((columns, n), bf16),
            full, full, full, full, full, full, full,
            pltpu.VMEM((rows, columns), f32),
            pltpu.VMEM((columns, n), f32),
            pltpu.VMEM((chips, share, n), f32),
            pltpu.VMEM((chips, share, n), f32),
            pltpu.VMEM((chips, share, n), f32),
            pltpu.VMEM((n, n), f32),
            pltpu.VMEM((n, n), f32),
            pltpu.VMEM((chips, n // 2, n), f32),
            pltpu.VMEM((n, 2 * n), f32),
            pltpu.VMEM((n, n), f32),
            dma((chunks,)), dma((chunks,)), dma((chunks,)), dma((chunks,)),
            dma((2,)), dma((chips,)), dma((chips,)), dma((2,)),
            dma((chips,)), dma((chips,)), dma((chips,)), dma((chips,)),
            dma((chips,)), dma((chips,)), dma((chips,)), dma((chips,)),
            dma((columns // n,)),
        ],
        compiler_params=pltpu.CompilerParams(
            collective_id=0, has_side_effects=True, vmem_limit_bytes=56 * 1024 * 1024
        ),
        cost_estimate=pl.CostEstimate(
            flops=20 * rows * n * columns, bytes_accessed=8 * rows * columns, transcendentals=0
        ),
    )(matrix, pivots[None, :], pivots[:, None], partner[None, :])

    tile = 2 * n
    trailing = pl.pallas_call(
        project,
        grid=(columns // tile,),
        out_shape=jax.ShapeDtypeStruct((rows, columns), f32),
        in_specs=[
            pl.BlockSpec((rows, tile), lambda i: (0, i)),
            pl.BlockSpec((rows, n), lambda i: (0, 0)),
            pl.BlockSpec((tile, n), lambda i: (i, 0)),
        ],
        out_specs=pl.BlockSpec((rows, tile), lambda i: (0, i)),
        compiler_params=pltpu.CompilerParams(vmem_limit_bytes=56 * 1024 * 1024),
    )(perm, w, summed)

    into = (spots[None, :] == pivots[:, None]) & (pivots[:, None] >= n)
    leading = spots[None, :] == positions[:, None]
    gone = jnp.any(into | leading, axis=0)
    moved = jnp.where(gone[None, :], 0.0, sketch) + jnp.dot(
        fronts_former, hot(jnp.concatenate([leading, into])), precision=highest
    )
    new_sketch = moved - jnp.dot(fronts_former[:, :n], solved, precision=highest)
    return (upper, trailing, new_sketch)


def solution(mesh):
    return jax.shard_map(
        functools.partial(per_device, mesh.shape["row"], mesh.shape["col"]),
        mesh=mesh,
        in_specs=(P("row", "col"), P(), P(None, ("col", "row"))),
        out_specs=(P(None, ("col", "row")), P("row", "col"), P(None, ("col", "row"))),
        check_vma=False,
    )
```

```python
import functools

import jax
import jax.numpy as jnp
from jax import lax
from jax.experimental import pallas as pl
from jax.experimental.pallas import tpu as pltpu
from jax.sharding import PartitionSpec as P

highest = lax.Precision.HIGHEST
f32 = jnp.float32
bf16 = jnp.bfloat16
MESH = pl.DeviceIdType.MESH
NN = (((1,), (0,)), ((), ()))
NT = (((1,), (1,)), ((), ()))
TN = (((0,), (0,)), ((), ()))


def dot(a, b, dims=NN, precision=None):
    return lax.dot_general(a, b, dims, precision=precision, preferred_element_type=f32)


def two(x):
    high = x.astype(bf16)
    return high, (x - high.astype(f32)).astype(bf16)


def three(x):
    high = x.astype(bf16)
    rest = x - high.astype(f32)
    mid = rest.astype(bf16)
    return high, mid, (rest - mid.astype(f32)).astype(bf16)


def dot3(a, b, dims=NN):
    (ah, al), (bh, bl) = a, b
    return dot(ah, bh, dims) + (dot(ah, bl, dims) + dot(al, bh, dims))


def pick3(parts, onehot):
    high, mid, low = parts
    return (dot(low, onehot) + dot(mid, onehot)) + dot(high, onehot)


def iota(shape, axis):
    return lax.broadcasted_iota(jnp.int32, shape, axis)


def cholesky_block(aug, linv, b, width):
    n = aug.shape[0]
    lo = b * width
    eye = jnp.where(iota((width, width), 0) == iota((width, width), 1), 1.0, 0.0).astype(f32)
    both = jnp.concatenate([aug[lo : lo + width, lo : lo + width], eye], axis=1)
    below = iota((width, 2 * width), 0)
    diag = jnp.ones((width, 2 * width), f32)
    for i in range(width):
        across = jnp.broadcast_to(both[:, i : i + 1], both.shape)
        pivot = across[i : i + 1, :]
        diag = jnp.where(below == i, pivot, diag)
        if i < width - 1:
            scaled = both[i : i + 1, :] * (1.0 / pivot)
            both = both - jnp.where(below > i, across, 0.0) * scaled
    inverse = both[:, width:] * lax.rsqrt(diag[:, :width])
    rows = dot3(two(inverse), two(aug[lo : lo + width, :]))
    linv[lo : lo + width, :] = rows[:, n:]
    if lo + width < n:
        start = (lo + width) // 128 * 128
        high, low = two(rows)
        left = (high[:, start:n], low[:, start:n])
        aug[start:, start:] = aug[start:, start:] - dot3(left, (high[:, start:], low[:, start:]), TN)


def kernel(
    nrow, ncol, chunks, width,
    x, pivots, sketch,
    perm_hbm, w_high, w_low, s_high, s_low, upper_out, sketch_out,
    onehot, picked, moved_in, from_left, from_right, to_right, to_left,
    panel, perm, product, summed, core_in, reduce_in, totals, gram, gram_in, gram_parts, aug, linv,
    sk_pad, sk_pick, sk_in, sk_part, sk_all,
    zr_s, zr_r, zl_s, zl_r, g1, g2_s, g2_r, g3, c_s, c_r, r_s, r_r, a_s, a_r, f_s, f_r, out_sem,
    ks_s, ks_r, kz_s, kz_r, ka_s, ka_r, kf_s, kf_r,
):
    rows, columns = x.shape
    n = panel.shape[1]
    tiles = columns // n
    chips = nrow // 2
    share = columns // nrow
    me = lax.axis_index("row")
    z = lax.axis_index("col")
    core = lax.rem(me, 2)
    chip = me // 2
    mate = me + 1 - 2 * core

    def remote(src, dst, ss, rs, dev):
        return pltpu.make_async_remote_copy(
            src_ref=src, dst_ref=dst, send_sem=ss, recv_sem=rs, device_id=dev, device_id_type=MESH
        )

    def peer(d):
        return lax.rem(chip + d, chips) * 2 + core

    def origin(d):
        return lax.rem(chip + chips - d, chips)

    def beside(d):
        return {"row": lax.rem(me + d, nrow)}

    def along(d):
        return {"col": lax.rem(z + d, ncol)}

    barrier = pltpu.get_barrier_semaphore()

    @pl.loop(1, nrow)
    def _(d):
        pl.semaphore_signal(barrier, inc=1, device_id=beside(d), device_id_type=MESH)

    @pl.loop(1, ncol)
    def _(d):
        pl.semaphore_signal(barrier, inc=1, device_id=along(d), device_id_type=MESH)

    def turned(row):
        return jnp.sum(jnp.where(iota((n, n), 0) == iota((n, n), 1), row, 0.0), axis=1, keepdims=True)

    row = pivots[...].astype(f32)
    col = turned(row)
    pos_row = iota((1, n), 1).astype(f32)
    pos_col = iota((n, 1), 0).astype(f32)
    absent_row = 1.0 - jnp.sum(jnp.where(col == pos_row, 1.0, 0.0), axis=0, keepdims=True)
    absent_col = 1.0 - jnp.sum(jnp.where(row == pos_col, 1.0, 0.0), axis=1, keepdims=True)
    rank_col = jnp.sum(jnp.where(pos_row < pos_col, absent_row, 0.0), axis=1, keepdims=True)
    rank_row = jnp.sum(jnp.where((col >= n) & (col < row), 1.0, 0.0), axis=0, keepdims=True)
    taken = jnp.where(rank_col == rank_row, absent_col * pos_col, 0.0)
    partner = jnp.sum(taken, axis=0, keepdims=True)
    piv_col = col.astype(jnp.int32)
    both_col = jnp.concatenate([piv_col, turned(partner).astype(jnp.int32)], axis=0)
    partner = partner.astype(jnp.int32)

    sk, pieces = sketch.shape
    slots = sk_pick.shape[0] // nrow
    spots = iota((1, pieces), 1) + (z * nrow + me) * pieces
    sk_pad[...] = jnp.zeros_like(sk_pad)
    sk_pad[:sk, :] = sketch[...]
    sk_hot = jnp.where(both_col == spots, 1.0, 0.0).astype(bf16)
    k_high, k_mid, k_low = three(sk_pad[...])
    sk_pick[...] = (dot(sk_hot, k_low, NT) + dot(sk_hot, k_mid, NT)) + dot(sk_hot, k_high, NT)

    def slots_of(owner):
        return pl.ds(pl.multiple_of(owner * slots, slots), slots)

    def sk_reduce(d):
        return remote(sk_pick.at[slots_of(lax.rem(me + d, nrow)), :], sk_in.at[d], ks_s.at[d], ks_r.at[d], beside(d))

    def sk_along(d):
        return remote(sk_part.at[0], sk_part.at[d], kz_s.at[d], kz_r.at[d], along(d))

    offset = z * columns
    local = pivots[...] - offset
    mine = (local >= 0) & (local < columns)
    before = local < 0

    @pl.loop(0, tiles)
    def _(t):
        at = pl.multiple_of(t * n, n)
        onehot[pl.ds(at, n), :] = jnp.where(iota((n, n), 0) + at == local, 1.0, 0.0).astype(bf16)

    pl.semaphore_wait(barrier, nrow + ncol - 2)

    @pl.loop(1, nrow)
    def _(d):
        sk_reduce(d).start()

    former_hot = jnp.where(iota((n, n), 0) == partner, 1.0, 0.0).astype(bf16)
    size = rows // chunks

    @pl.loop(0, chunks)
    def _(c):
        at = pl.ds(pl.multiple_of(c * size, size), size)
        picked[at, :] = pick3(three(x[at, :]), onehot[...])

    @pl.when(z == 0)
    def _():
        @pl.loop(0, chunks)
        def _(c):
            at = pl.ds(pl.multiple_of(c * size, size), size)
            moved_in[at, :] = pick3(three(x[at, :n]), former_hot)

    def right(c):
        at = pl.ds(pl.multiple_of(c * size, size), size)
        return remote(to_right.at[at, :], from_left.at[at, :], zr_s.at[c], zr_r.at[c], {"col": z + 1})

    def left(c):
        at = pl.ds(pl.multiple_of(c * size, size), size)
        return remote(to_left.at[at, :], from_right.at[at, :], zl_s.at[c], zl_r.at[c], {"col": z - 1})

    @pl.loop(0, chunks + ncol - 1)
    def _(t):
        c = t - z

        @pl.when((c >= 0) & (c < chunks))
        def _():
            at = pl.ds(pl.multiple_of(c * size, size), size)

            @pl.when(z > 0)
            def _():
                right(c).wait_recv()
                moved_in[at, :] = from_left[at, :]

            @pl.when(z < ncol - 1)
            def _():
                to_right[at, :] = jnp.where(mine, picked[at, :], moved_in[at, :])
                right(c).start()

        e = t - (ncol - 1 - z)

        @pl.when((e >= 0) & (e < chunks))
        def _():
            at = pl.ds(pl.multiple_of(e * size, size), size)

            @pl.when(z < ncol - 1)
            def _():
                left(e).wait_recv()
                panel[at, :] = jnp.where(mine, picked[at, :], from_right[at, :])

            @pl.when(z == ncol - 1)
            def _():
                panel[at, :] = picked[at, :]

            @pl.when(z > 0)
            def _():
                to_left[at, :] = panel[at, :]
                left(e).start()

    panel[...] = jnp.where(before, moved_in[...], panel[...])

    half = n // 2
    columns_of = panel[...].T
    gram[...] = dot(columns_of, panel[...], precision=highest)
    first = remote(gram, gram_in, g1.at[0], g1.at[1], {"row": mate})
    first.start()

    left_parts = two(columns_of)
    former = three(moved_in[...])
    wanted = piv_col - offset
    usable = piv_col >= n

    first.wait()
    mine_rows = pl.ds(pl.multiple_of(core * half, half), half)
    other_rows = pl.ds(pl.multiple_of((1 - core) * half, half), half)
    gram_parts[0, :, :] = gram[mine_rows, :] + gram_in[mine_rows, :]

    def gram_to(d):
        return remote(gram_parts.at[0], gram_parts.at[d], g2_s.at[d], g2_r.at[d], {"row": peer(d)})

    for d in range(1, chips):
        gram_to(d).start()

    def out_copy(t):
        at = pl.ds(pl.multiple_of(t * n, n), n)
        return pltpu.make_async_copy(perm.at[:, at], perm_hbm.at[:, at], out_sem.at[t])

    @pl.loop(0, tiles)
    def _(t):
        at = pl.multiple_of(t * n, n)
        place = (iota((n, n), 1) + at == wanted) & usable
        place = jnp.where(place, 1.0, 0.0)
        keep = 1.0 - jnp.sum(place, axis=0, keepdims=True)
        tile = x[:, pl.ds(at, n)] * keep + pick3(former, place.astype(bf16))
        tile = jnp.where((z == 0) & (t == 0), panel[...], tile)
        perm[:, pl.ds(at, n)] = tile
        out_copy(t).start()
        product[pl.ds(at, n), :] = dot3(left_parts, two(tile)).T

    def part(owner):
        return pl.ds(pl.multiple_of(owner * share, share), share)

    def to_mate(c):
        return remote(product.at[part(2 * c + 1 - core), :], core_in.at[c], c_s.at[c], c_r.at[c], {"row": mate})

    for c in range(chips):
        to_mate(c).start()

    for c in range(chips):
        to_mate(c).wait()
        totals[c, :, :] = product[part(2 * c + core), :] + core_in[c, :, :]

    def reduce_to(d):
        return remote(totals.at[lax.rem(chip + d, chips)], reduce_in.at[d], r_s.at[d], r_r.at[d], {"row": peer(d)})

    for d in range(1, chips):
        reduce_to(d).start()

    @pl.loop(1, nrow)
    def _(d):
        sk_reduce(d).wait()

    sk_part[0, :, :] = sk_pick[slots_of(me), :] + jnp.sum(sk_in[1:, :, :], axis=0)
    for d in range(1, ncol):
        sk_along(d).start()

    for d in range(1, chips):
        gram_to(d).wait()
    gram_half = jnp.zeros((half, n), f32)
    for d in range(chips):
        gram_half = gram_half + gram_parts[lax.rem(chip + chips - d, chips), :, :]
    aug[mine_rows, :n] = gram_half
    last = remote(aug.at[mine_rows, :n], aug.at[mine_rows, :n], g3.at[0], g3.at[1], {"row": mate})
    last.start()
    aug[:, n:] = jnp.where(iota((n, n), 0) == iota((n, n), 1), 1.0, 0.0).astype(f32)
    last.wait_send()
    remote(aug.at[other_rows, :n], aug.at[other_rows, :n], g3.at[0], g3.at[1], {"row": mate}).wait_recv()

    def gather_to(d):
        return remote(summed.at[part(me), :], summed.at[part(me), :], a_s.at[d], a_r.at[d], {"row": peer(d)})

    def gathered(d):
        at = part(origin(d) * 2 + core)
        return remote(summed.at[at, :], summed.at[at, :], a_s.at[d], a_r.at[d], {"row": peer(d)})

    def forward(d):
        at = part(origin(d) * 2 + core)
        return remote(summed.at[at, :], summed.at[at, :], f_s.at[d], f_r.at[d], {"row": mate})

    def forwarded(d):
        at = part(origin(d) * 2 + 1 - core)
        return remote(summed.at[at, :], summed.at[at, :], f_s.at[d], f_r.at[d], {"row": mate})

    def sk_gather_to(d):
        at = slots_of(me)
        return remote(sk_all.at[at, :], sk_all.at[at, :], ka_s.at[d], ka_r.at[d], {"row": peer(d)})

    def sk_gathered(d):
        at = slots_of(origin(d) * 2 + core)
        return remote(sk_all.at[at, :], sk_all.at[at, :], ka_s.at[d], ka_r.at[d], {"row": peer(d)})

    def sk_forward(d):
        at = slots_of(origin(d) * 2 + core)
        return remote(sk_all.at[at, :], sk_all.at[at, :], kf_s.at[d], kf_r.at[d], {"row": mate})

    def sk_forwarded(d):
        at = slots_of(origin(d) * 2 + 1 - core)
        return remote(sk_all.at[at, :], sk_all.at[at, :], kf_s.at[d], kf_r.at[d], {"row": mate})

    def finish_reduce():
        total = totals[chip, :, :]
        for d in range(1, chips):
            reduce_to(d).wait()
            total = total + reduce_in[d, :, :]
        summed[part(me), :] = total
        for d in range(1, chips):
            gather_to(d).start()
        forward(0).start()
        for d in range(1, ncol):
            sk_along(d).wait()
        sk_all[slots_of(me), :] = jnp.sum(sk_part[...], axis=0)
        for d in range(1, chips):
            sk_gather_to(d).start()
        sk_forward(0).start()

    def finish_gather():
        for d in range(1, chips):
            gathered(d).wait_recv()
            forward(d).start()

    blocks = n // width
    for b in range(blocks):
        cholesky_block(aug, linv, b, width)
        if b == blocks // 2 - 1:
            finish_reduce()
    finish_gather()
    for d in range(1, chips):
        sk_gathered(d).wait_recv()
        sk_forward(d).start()

    inverse = dot3(two(linv[...]), two(linv[...]), TN)
    w_high[...], w_low[...] = two(dot3(two(panel[...]), two(inverse)))
    own = two(summed[part(me), :])
    upper_out[...] = dot3(two(linv[...]), own, NT)
    solved = dot3(two(inverse), own, NT)

    for d in range(chips):
        forwarded(d).wait_recv()

    @pl.loop(0, tiles)
    def _(t):
        at = pl.ds(pl.multiple_of(t * n, n), n)
        high, low = two(summed[at, :].T)
        s_high[:, at] = high
        s_low[:, at] = low

    for d in range(chips):
        sk_forwarded(d).wait_recv()
    into = jnp.where((spots == piv_col) & (piv_col >= n), 1.0, 0.0)
    leading = jnp.where(spots == iota((n, 1), 0), 1.0, 0.0)
    chosen = jnp.concatenate([leading, into], axis=0)
    stay = 1.0 - jnp.sum(chosen, axis=0, keepdims=True)
    turned_all = sk_all[...].T
    changed = pick3(three(turned_all), chosen.astype(bf16)) - dot3(two(turned_all[:, :n]), two(solved))
    sketch_out[...] = sketch[...] * stay + changed[:sk, :]

    for d in range(1, chips):
        gather_to(d).wait_send()
        sk_gather_to(d).wait_send()
    for d in range(chips):
        forward(d).wait_send()
        sk_forward(d).wait_send()

    @pl.loop(0, chunks)
    def _(c):
        @pl.when(z < ncol - 1)
        def _():
            right(c).wait_send()

        @pl.when(z > 0)
        def _():
            left(c).wait_send()

    @pl.loop(0, tiles)
    def _(t):
        out_copy(t).wait()


def project(perm, w_high, w_low, s_high, s_low, out):
    out[...] = perm[...] - dot3((w_high[...], w_low[...]), (s_high[...], s_low[...]))


def per_device(nrow, ncol, matrix, pivots, sketch):
    rows, columns = matrix.shape
    n = pivots.shape[0]
    sk, pieces = sketch.shape
    padded = (sk + 127) // 128 * 128
    chunks = 10
    width = 64
    chips = nrow // 2
    share = columns // nrow
    slots = 2 * n // nrow
    vmem = pl.BlockSpec(memory_space=pltpu.VMEM)
    full = pltpu.VMEM((rows, n), f32)
    dma = pltpu.SemaphoreType.DMA
    shape = jax.ShapeDtypeStruct
    perm, w_high, w_low, s_high, s_low, upper, new_sketch = pl.pallas_call(
        functools.partial(kernel, nrow, ncol, chunks, width),
        out_shape=[
            shape((rows, columns), f32),
            shape((rows, n), bf16),
            shape((rows, n), bf16),
            shape((n, columns), bf16),
            shape((n, columns), bf16),
            shape((n, share), f32),
            shape((sk, pieces), f32),
        ],
        in_specs=[vmem] * 3,
        out_specs=[pl.BlockSpec(memory_space=pl.ANY)] + [vmem] * 6,
        scratch_shapes=[
            pltpu.VMEM((columns, n), bf16),
            full, full, full, full, full, full, full,
            pltpu.VMEM((rows, columns), f32),
            pltpu.VMEM((columns, n), f32),
            pltpu.VMEM((columns, n), f32),
            pltpu.VMEM((chips, share, n), f32),
            pltpu.VMEM((chips, share, n), f32),
            pltpu.VMEM((chips, share, n), f32),
            pltpu.VMEM((n, n), f32),
            pltpu.VMEM((n, n), f32),
            pltpu.VMEM((chips, n // 2, n), f32),
            pltpu.VMEM((n, 2 * n), f32),
            pltpu.VMEM((n, n), f32),
            pltpu.VMEM((padded, pieces), f32),
            pltpu.VMEM((2 * n, padded), f32),
            pltpu.VMEM((nrow, slots, padded), f32),
            pltpu.VMEM((ncol, slots, padded), f32),
            pltpu.VMEM((2 * n, padded), f32),
            dma((chunks,)), dma((chunks,)), dma((chunks,)), dma((chunks,)),
            dma((2,)), dma((chips,)), dma((chips,)), dma((2,)),
            dma((chips,)), dma((chips,)), dma((chips,)), dma((chips,)),
            dma((chips,)), dma((chips,)), dma((chips,)), dma((chips,)),
            dma((columns // n,)),
            dma((nrow,)), dma((nrow,)), dma((ncol,)), dma((ncol,)),
            dma((chips,)), dma((chips,)), dma((chips,)), dma((chips,)),
        ],
        compiler_params=pltpu.CompilerParams(
            collective_id=0, has_side_effects=True, vmem_limit_bytes=56 * 1024 * 1024
        ),
        cost_estimate=pl.CostEstimate(
            flops=20 * rows * n * columns, bytes_accessed=8 * rows * columns, transcendentals=0
        ),
    )(matrix, pivots[None, :], sketch)

    tile = 2 * n
    whole = pl.BlockSpec((rows, n), lambda i: (0, 0))
    across = pl.BlockSpec((n, tile), lambda i: (0, i))
    trailing = pl.pallas_call(
        project,
        grid=(columns // tile,),
        out_shape=jax.ShapeDtypeStruct((rows, columns), f32),
        in_specs=[pl.BlockSpec((rows, tile), lambda i: (0, i)), whole, whole, across, across],
        out_specs=pl.BlockSpec((rows, tile), lambda i: (0, i)),
        compiler_params=pltpu.CompilerParams(vmem_limit_bytes=56 * 1024 * 1024),
    )(perm, w_high, w_low, s_high, s_low)
    return (upper, trailing, new_sketch)


def solution(mesh):
    return jax.shard_map(
        functools.partial(per_device, mesh.shape["row"], mesh.shape["col"]),
        mesh=mesh,
        in_specs=(P("row", "col"), P(), P(None, ("col", "row"))),
        out_specs=(P(None, ("col", "row")), P("row", "col"), P(None, ("col", "row"))),
        check_vma=False,
    )
```

```python
import functools

import jax
import jax.numpy as jnp
from jax import lax
from jax.experimental import pallas as pl
from jax.experimental.pallas import tpu as pltpu
from jax.sharding import PartitionSpec as P

highest = lax.Precision.HIGHEST
f32 = jnp.float32
bf16 = jnp.bfloat16
MESH = pl.DeviceIdType.MESH
NN = (((1,), (0,)), ((), ()))
NT = (((1,), (1,)), ((), ()))
TN = (((0,), (0,)), ((), ()))


def dot(a, b, dims=NN, precision=None):
    return lax.dot_general(a, b, dims, precision=precision, preferred_element_type=f32)


def two(x):
    high = x.astype(bf16)
    return high, (x - high.astype(f32)).astype(bf16)


def three(x):
    high = x.astype(bf16)
    rest = x - high.astype(f32)
    mid = rest.astype(bf16)
    return high, mid, (rest - mid.astype(f32)).astype(bf16)


def dot3(a, b, dims=NN):
    (ah, al), (bh, bl) = a, b
    ((i,), (j,)), _ = dims
    if ah.shape[i] % 64 == 0:
        left = jnp.concatenate([al, ah, ah], axis=i)
        return dot(left, jnp.concatenate([bh, bl, bh], axis=j), dims)
    return dot(ah, bh, dims) + (dot(ah, bl, dims) + dot(al, bh, dims))


def pick3(parts, onehot):
    high, mid, low = parts
    left = jnp.concatenate([low, mid, high], axis=1)
    return dot(left, jnp.concatenate([onehot] * 3, axis=0))


def iota(shape, axis):
    return lax.broadcasted_iota(jnp.int32, shape, axis)


def cholesky_block(aug, linv, b, width):
    n = aug.shape[0]
    lo = b * width
    eye = jnp.where(iota((width, width), 0) == iota((width, width), 1), 1.0, 0.0).astype(f32)
    both = jnp.concatenate([aug[lo : lo + width, lo : lo + width], eye], axis=1)
    below = iota((width, 2 * width), 0)
    diag = jnp.ones((width, 2 * width), f32)
    group = 4
    for first in range(0, width, group):
        across = [
            jnp.broadcast_to(both[:, i : i + 1], both.shape) for i in range(first, first + group)
        ]
        for k in range(group):
            i = first + k
            inv = 1.0 / across[k][i : i + 1, :]
            diag = jnp.where(below == i, inv, diag)
            scaled = both[i : i + 1, :] * inv
            column = jnp.where(below > i, across[k], 0.0)
            for l in range(k + 1, group):
                across[l] = across[l] - column * (across[l][i : i + 1, :] * inv)
            both = both - column * scaled
    inverse = both[:, width:] * jnp.sqrt(diag[:, :width])
    rows = dot3(two(inverse), two(aug[lo : lo + width, :]))
    linv[lo : lo + width, :] = rows[:, n:]
    if lo + width < n:
        start = (lo + width) // 128 * 128
        high, low = two(rows)
        left = (high[:, start:n], low[:, start:n])
        aug[start:, start:] = aug[start:, start:] - dot3(left, (high[:, start:], low[:, start:]), TN)


def kernel(
    nrow, ncol, chunks, skew, width,
    x, pivots, sketch,
    perm_hbm, w_high, w_low, s_high, s_low, upper_out, sketch_out,
    picked, moved_in, from_left, from_right, to_right, to_left,
    panel, perm, product, summed, core_in, reduce_in, totals, gram, gram_in, gram_parts, aug, linv,
    sk_pad, sk_pick, sk_in, sk_part, sk_all,
    zr_s, zr_r, zl_s, zl_r, g1, g2_s, g2_r, g3, c_s, c_r, r_s, r_r, a_s, a_r, f_s, f_r, out_sem,
    ks_s, ks_r, kz_s, kz_r, ka_s, ka_r, kf_s, kf_r,
):
    rows, columns = x.shape
    n = panel.shape[1]
    tiles = columns // n
    chips = nrow // 2
    share = columns // nrow
    me = lax.axis_index("row")
    z = lax.axis_index("col")
    core = lax.rem(me, 2)
    chip = me // 2
    mate = me + 1 - 2 * core

    def remote(src, dst, ss, rs, dev):
        return pltpu.make_async_remote_copy(
            src_ref=src, dst_ref=dst, send_sem=ss, recv_sem=rs, device_id=dev, device_id_type=MESH
        )

    def peer(d):
        return lax.rem(chip + d, chips) * 2 + core

    def origin(d):
        return lax.rem(chip + chips - d, chips)

    def beside(d):
        return {"row": lax.rem(me + d, nrow)}

    def along(d):
        return {"col": lax.rem(z + d, ncol)}

    barrier = pltpu.get_barrier_semaphore()

    @pl.loop(1, nrow)
    def _(d):
        pl.semaphore_signal(barrier, inc=1, device_id=beside(d), device_id_type=MESH)

    @pl.loop(1, ncol)
    def _(d):
        pl.semaphore_signal(barrier, inc=1, device_id=along(d), device_id_type=MESH)

    def turned(row):
        return jnp.sum(jnp.where(iota((n, n), 0) == iota((n, n), 1), row, 0.0), axis=1, keepdims=True)

    row = pivots[...].astype(f32)
    col = turned(row)
    pos_row = iota((1, n), 1).astype(f32)
    pos_col = iota((n, 1), 0).astype(f32)
    absent_row = 1.0 - jnp.sum(jnp.where(col == pos_row, 1.0, 0.0), axis=0, keepdims=True)
    absent_col = 1.0 - jnp.sum(jnp.where(row == pos_col, 1.0, 0.0), axis=1, keepdims=True)
    rank_col = jnp.sum(jnp.where(pos_row < pos_col, absent_row, 0.0), axis=1, keepdims=True)
    rank_row = jnp.sum(jnp.where((col >= n) & (col < row), 1.0, 0.0), axis=0, keepdims=True)
    taken = jnp.where(rank_col == rank_row, absent_col * pos_col, 0.0)
    partner = jnp.sum(taken, axis=0, keepdims=True)
    piv_col = col.astype(jnp.int32)
    both_col = jnp.concatenate([piv_col, turned(partner).astype(jnp.int32)], axis=0)
    partner = partner.astype(jnp.int32)

    sk, pieces = sketch.shape
    slots = sk_pick.shape[0] // nrow
    spots = iota((1, pieces), 1) + (z * nrow + me) * pieces
    sk_pad[...] = jnp.zeros_like(sk_pad)
    sk_pad[:sk, :] = sketch[...]
    sk_hot = jnp.where(both_col == spots, 1.0, 0.0).astype(bf16)
    k_high, k_mid, k_low = three(sk_pad[...])
    sk_pick[...] = (dot(sk_hot, k_low, NT) + dot(sk_hot, k_mid, NT)) + dot(sk_hot, k_high, NT)

    def slots_of(owner):
        return pl.ds(pl.multiple_of(owner * slots, slots), slots)

    def sk_reduce(d):
        return remote(sk_pick.at[slots_of(lax.rem(me + d, nrow)), :], sk_in.at[d], ks_s.at[d], ks_r.at[d], beside(d))

    def sk_along(d):
        return remote(sk_part.at[0], sk_part.at[d], kz_s.at[d], kz_r.at[d], along(d))

    offset = z * columns
    local = pivots[...] - offset
    mine = (local >= 0) & (local < columns)
    before = local < 0

    pl.semaphore_wait(barrier, nrow + ncol - 2)

    @pl.loop(1, nrow)
    def _(d):
        sk_reduce(d).start()

    former_hot = jnp.where(iota((n, n), 0) == partner, 1.0, 0.0).astype(bf16)
    size = rows // chunks

    picked[...] = jnp.zeros_like(picked)

    @pl.loop(0, tiles)
    def _(t):
        at = pl.multiple_of(t * n, n)
        onehot = jnp.where(iota((n, n), 0) + at == local, 1.0, 0.0).astype(bf16)
        picked[...] += pick3(three(x[:, pl.ds(at, n)]), onehot)

    @pl.when(z == 0)
    def _():
        moved_in[...] = pick3(three(x[:, :n]), former_hot)

    def right(c):
        at = pl.ds(pl.multiple_of(c * size, size), size)
        return remote(to_right.at[at, :], from_left.at[at, :], zr_s.at[c], zr_r.at[c], {"col": z + 1})

    def left(c):
        at = pl.ds(pl.multiple_of(c * size, size), size)
        return remote(to_left.at[at, :], from_right.at[at, :], zl_s.at[c], zl_r.at[c], {"col": z - 1})

    @pl.loop(0, chunks + skew * (ncol - 1))
    def _(t):
        c = t - skew * z

        @pl.when((c >= 0) & (c < chunks))
        def _():
            at = pl.ds(pl.multiple_of(c * size, size), size)

            @pl.when(z > 0)
            def _():
                right(c).wait_recv()
                moved_in[at, :] = from_left[at, :]

            @pl.when(z < ncol - 1)
            def _():
                to_right[at, :] = jnp.where(mine, picked[at, :], moved_in[at, :])
                right(c).start()

        e = t - skew * (ncol - 1 - z)

        @pl.when((e >= 0) & (e < chunks))
        def _():
            at = pl.ds(pl.multiple_of(e * size, size), size)

            @pl.when(z < ncol - 1)
            def _():
                left(e).wait_recv()
                panel[at, :] = jnp.where(mine, picked[at, :], from_right[at, :])

            @pl.when(z == ncol - 1)
            def _():
                panel[at, :] = picked[at, :]

            @pl.when(z > 0)
            def _():
                to_left[at, :] = panel[at, :]
                left(e).start()

    panel[...] = jnp.where(before, moved_in[...], panel[...])

    half = n // 2
    columns_of = panel[...].T
    gram[...] = dot(columns_of, panel[...], precision=highest)
    first = remote(gram, gram_in, g1.at[0], g1.at[1], {"row": mate})
    first.start()

    left_parts = two(columns_of)
    former = three(moved_in[...])
    wanted = piv_col - offset
    usable = piv_col >= n

    first.wait()
    mine_rows = pl.ds(pl.multiple_of(core * half, half), half)
    other_rows = pl.ds(pl.multiple_of((1 - core) * half, half), half)
    gram_parts[0, :, :] = gram[mine_rows, :] + gram_in[mine_rows, :]

    def gram_to(d):
        return remote(gram_parts.at[0], gram_parts.at[d], g2_s.at[d], g2_r.at[d], {"row": peer(d)})

    for d in range(1, chips):
        gram_to(d).start()

    def out_copy(t):
        at = pl.ds(pl.multiple_of(t * n, n), n)
        return pltpu.make_async_copy(perm.at[:, at], perm_hbm.at[:, at], out_sem.at[t])

    @pl.loop(0, tiles)
    def _(t):
        at = pl.multiple_of(t * n, n)
        place = (iota((n, n), 1) + at == wanted) & usable
        place = jnp.where(place, 1.0, 0.0)
        keep = 1.0 - jnp.sum(place, axis=0, keepdims=True)
        tile = x[:, pl.ds(at, n)] * keep + pick3(former, place.astype(bf16))
        tile = jnp.where((z == 0) & (t == 0), panel[...], tile)
        perm[:, pl.ds(at, n)] = tile
        out_copy(t).start()
        product[pl.ds(at, n), :] = dot3(left_parts, two(tile)).T

    def part(owner):
        return pl.ds(pl.multiple_of(owner * share, share), share)

    def to_mate(c):
        return remote(product.at[part(2 * c + 1 - core), :], core_in.at[c], c_s.at[c], c_r.at[c], {"row": mate})

    for c in range(chips):
        to_mate(c).start()

    for c in range(chips):
        to_mate(c).wait()
        totals[c, :, :] = product[part(2 * c + core), :] + core_in[c, :, :]

    def reduce_to(d):
        return remote(totals.at[lax.rem(chip + d, chips)], reduce_in.at[d], r_s.at[d], r_r.at[d], {"row": peer(d)})

    for d in range(1, chips):
        reduce_to(d).start()

    @pl.loop(1, nrow)
    def _(d):
        sk_reduce(d).wait()

    sk_part[0, :, :] = sk_pick[slots_of(me), :] + jnp.sum(sk_in[1:, :, :], axis=0)
    for d in range(1, ncol):
        sk_along(d).start()

    for d in range(1, chips):
        gram_to(d).wait()
    gram_half = jnp.zeros((half, n), f32)
    for d in range(chips):
        gram_half = gram_half + gram_parts[lax.rem(chip + chips - d, chips), :, :]
    aug[mine_rows, :n] = gram_half
    last = remote(aug.at[mine_rows, :n], aug.at[mine_rows, :n], g3.at[0], g3.at[1], {"row": mate})
    last.start()
    aug[:, n:] = jnp.where(iota((n, n), 0) == iota((n, n), 1), 1.0, 0.0).astype(f32)
    last.wait_send()
    remote(aug.at[other_rows, :n], aug.at[other_rows, :n], g3.at[0], g3.at[1], {"row": mate}).wait_recv()

    def gather_to(d):
        return remote(summed.at[part(me), :], summed.at[part(me), :], a_s.at[d], a_r.at[d], {"row": peer(d)})

    def gathered(d):
        at = part(origin(d) * 2 + core)
        return remote(summed.at[at, :], summed.at[at, :], a_s.at[d], a_r.at[d], {"row": peer(d)})

    def forward(d):
        at = part(origin(d) * 2 + core)
        return remote(summed.at[at, :], summed.at[at, :], f_s.at[d], f_r.at[d], {"row": mate})

    def forwarded(d):
        at = part(origin(d) * 2 + 1 - core)
        return remote(summed.at[at, :], summed.at[at, :], f_s.at[d], f_r.at[d], {"row": mate})

    def sk_gather_to(d):
        at = slots_of(me)
        return remote(sk_all.at[at, :], sk_all.at[at, :], ka_s.at[d], ka_r.at[d], {"row": peer(d)})

    def sk_gathered(d):
        at = slots_of(origin(d) * 2 + core)
        return remote(sk_all.at[at, :], sk_all.at[at, :], ka_s.at[d], ka_r.at[d], {"row": peer(d)})

    def sk_forward(d):
        at = slots_of(origin(d) * 2 + core)
        return remote(sk_all.at[at, :], sk_all.at[at, :], kf_s.at[d], kf_r.at[d], {"row": mate})

    def sk_forwarded(d):
        at = slots_of(origin(d) * 2 + 1 - core)
        return remote(sk_all.at[at, :], sk_all.at[at, :], kf_s.at[d], kf_r.at[d], {"row": mate})

    def finish_reduce():
        total = totals[chip, :, :]
        for d in range(1, chips):
            reduce_to(d).wait()
            total = total + reduce_in[d, :, :]
        summed[part(me), :] = total
        for d in range(1, chips):
            gather_to(d).start()
        forward(0).start()
        for d in range(1, ncol):
            sk_along(d).wait()
        sk_all[slots_of(me), :] = jnp.sum(sk_part[...], axis=0)
        for d in range(1, chips):
            sk_gather_to(d).start()
        sk_forward(0).start()

    def finish_gather():
        for d in range(1, chips):
            gathered(d).wait_recv()
            forward(d).start()

    blocks = n // width
    for b in range(blocks):
        cholesky_block(aug, linv, b, width)
        if b == blocks // 2 - 1:
            finish_reduce()
    finish_gather()
    for d in range(1, chips):
        sk_gathered(d).wait_recv()
        sk_forward(d).start()

    inverse = dot3(two(linv[...]), two(linv[...]), TN)
    w_high[...], w_low[...] = two(dot3(two(panel[...]), two(inverse)))
    own = two(summed[part(me), :])
    upper_out[...] = dot3(two(linv[...]), own, NT)
    solved = dot3(two(inverse), own, NT)

    for d in range(chips):
        forwarded(d).wait_recv()

    @pl.loop(0, tiles)
    def _(t):
        at = pl.ds(pl.multiple_of(t * n, n), n)
        high, low = two(summed[at, :].T)
        s_high[:, at] = high
        s_low[:, at] = low

    for d in range(chips):
        sk_forwarded(d).wait_recv()
    into = jnp.where((spots == piv_col) & (piv_col >= n), 1.0, 0.0)
    leading = jnp.where(spots == iota((n, 1), 0), 1.0, 0.0)
    chosen = jnp.concatenate([leading, into], axis=0)
    stay = 1.0 - jnp.sum(chosen, axis=0, keepdims=True)
    turned_all = sk_all[...].T
    changed = pick3(three(turned_all), chosen.astype(bf16)) - dot3(two(turned_all[:, :n]), two(solved))
    sketch_out[...] = sketch[...] * stay + changed[:sk, :]

    for d in range(1, chips):
        gather_to(d).wait_send()
        sk_gather_to(d).wait_send()
    for d in range(chips):
        forward(d).wait_send()
        sk_forward(d).wait_send()

    @pl.loop(0, chunks)
    def _(c):
        @pl.when(z < ncol - 1)
        def _():
            right(c).wait_send()

        @pl.when(z > 0)
        def _():
            left(c).wait_send()

    @pl.loop(0, tiles)
    def _(t):
        out_copy(t).wait()


def project(perm, w_high, w_low, s_high, s_low, upper, sketch, out, upper_out, sketch_out):
    @pl.when(pl.program_id(0) == 0)
    def _():
        upper_out[...] = upper[...]
        sketch_out[...] = sketch[...]

    out[...] = perm[...] - dot3((w_high[...], w_low[...]), (s_high[...], s_low[...]))


def per_device(nrow, ncol, matrix, pivots, sketch):
    rows, columns = matrix.shape
    n = pivots.shape[0]
    sk, pieces = sketch.shape
    padded = (sk + 127) // 128 * 128
    chunks = 20
    skew = 3
    width = 64
    chips = nrow // 2
    share = columns // nrow
    slots = 2 * n // nrow
    vmem = pl.BlockSpec(memory_space=pltpu.VMEM)
    full = pltpu.VMEM((rows, n), f32)
    dma = pltpu.SemaphoreType.DMA
    shape = jax.ShapeDtypeStruct
    perm, w_high, w_low, s_high, s_low, upper, new_sketch = pl.pallas_call(
        functools.partial(kernel, nrow, ncol, chunks, skew, width),
        out_shape=[
            shape((rows, columns), f32),
            shape((rows, n), bf16),
            shape((rows, n), bf16),
            shape((n, columns), bf16),
            shape((n, columns), bf16),
            shape((n, share), f32),
            shape((sk, pieces), f32),
        ],
        in_specs=[vmem] * 3,
        out_specs=[pl.BlockSpec(memory_space=pl.ANY)] + [vmem] * 6,
        scratch_shapes=[
            full, full, full, full, full, full, full,
            pltpu.VMEM((rows, columns), f32),
            pltpu.VMEM((columns, n), f32),
            pltpu.VMEM((columns, n), f32),
            pltpu.VMEM((chips, share, n), f32),
            pltpu.VMEM((chips, share, n), f32),
            pltpu.VMEM((chips, share, n), f32),
            pltpu.VMEM((n, n), f32),
            pltpu.VMEM((n, n), f32),
            pltpu.VMEM((chips, n // 2, n), f32),
            pltpu.VMEM((n, 2 * n), f32),
            pltpu.VMEM((n, n), f32),
            pltpu.VMEM((padded, pieces), f32),
            pltpu.VMEM((2 * n, padded), f32),
            pltpu.VMEM((nrow, slots, padded), f32),
            pltpu.VMEM((ncol, slots, padded), f32),
            pltpu.VMEM((2 * n, padded), f32),
            dma((chunks,)), dma((chunks,)), dma((chunks,)), dma((chunks,)),
            dma((2,)), dma((chips,)), dma((chips,)), dma((2,)),
            dma((chips,)), dma((chips,)), dma((chips,)), dma((chips,)),
            dma((chips,)), dma((chips,)), dma((chips,)), dma((chips,)),
            dma((columns // n,)),
            dma((nrow,)), dma((nrow,)), dma((ncol,)), dma((ncol,)),
            dma((chips,)), dma((chips,)), dma((chips,)), dma((chips,)),
        ],
        compiler_params=pltpu.CompilerParams(
            collective_id=0, has_side_effects=True, vmem_limit_bytes=56 * 1024 * 1024
        ),
        cost_estimate=pl.CostEstimate(
            flops=20 * rows * n * columns, bytes_accessed=8 * rows * columns, transcendentals=0
        ),
    )(matrix, pivots[None, :], sketch)

    tile = 2 * n
    whole = pl.BlockSpec((rows, n), lambda i: (0, 0))
    across = pl.BlockSpec((n, tile), lambda i: (0, i))
    small = [pl.BlockSpec(a.shape, lambda i: (0, 0)) for a in (upper, new_sketch)]
    trailing, upper, new_sketch = pl.pallas_call(
        project,
        grid=(columns // tile,),
        out_shape=[shape((rows, columns), f32), shape(upper.shape, f32), shape(new_sketch.shape, f32)],
        in_specs=[pl.BlockSpec((rows, tile), lambda i: (0, i)), whole, whole, across, across]
        + small,
        out_specs=[pl.BlockSpec((rows, tile), lambda i: (0, i))] + small,
        compiler_params=pltpu.CompilerParams(vmem_limit_bytes=56 * 1024 * 1024),
    )(perm, w_high, w_low, s_high, s_low, upper, new_sketch)
    return (upper, trailing, new_sketch)


def solution(mesh):
    return jax.shard_map(
        functools.partial(per_device, mesh.shape["row"], mesh.shape["col"]),
        mesh=mesh,
        in_specs=(P("row", "col"), P(), P(None, ("col", "row"))),
        out_specs=(P(None, ("col", "row")), P("row", "col"), P(None, ("col", "row"))),
        check_vma=False,
    )
```

```python
import functools

import jax
import jax.numpy as jnp
from jax import lax
from jax.experimental import pallas as pl
from jax.experimental.pallas import tpu as pltpu
from jax.sharding import PartitionSpec as P

highest = lax.Precision.HIGHEST
f32 = jnp.float32
bf16 = jnp.bfloat16
MESH = pl.DeviceIdType.MESH
NN = (((1,), (0,)), ((), ()))
NT = (((1,), (1,)), ((), ()))
TN = (((0,), (0,)), ((), ()))


def dot(a, b, dims=NN, precision=None):
    return lax.dot_general(a, b, dims, precision=precision, preferred_element_type=f32)


def two(x):
    high = x.astype(bf16)
    return high, (x - high.astype(f32)).astype(bf16)


def three(x):
    high = x.astype(bf16)
    rest = x - high.astype(f32)
    mid = rest.astype(bf16)
    return high, mid, (rest - mid.astype(f32)).astype(bf16)


def dot3(a, b, dims=NN):
    (ah, al), (bh, bl) = a, b
    ((i,), (j,)), _ = dims
    if ah.shape[i] % 64 == 0:
        left = jnp.concatenate([al, ah, ah], axis=i)
        return dot(left, jnp.concatenate([bh, bl, bh], axis=j), dims)
    return dot(ah, bh, dims) + (dot(ah, bl, dims) + dot(al, bh, dims))


def pick3(parts, onehot):
    high, mid, low = parts
    left = jnp.concatenate([low, mid, high], axis=1)
    return dot(left, jnp.concatenate([onehot] * 3, axis=0))


def iota(shape, axis):
    return lax.broadcasted_iota(jnp.int32, shape, axis)


def cholesky_block(aug, linv, b, width):
    n = aug.shape[0]
    lo = b * width
    eye = jnp.where(iota((width, width), 0) == iota((width, width), 1), 1.0, 0.0).astype(f32)
    both = jnp.concatenate([aug[lo : lo + width, lo : lo + width], eye], axis=1)
    below = iota((width, 2 * width), 0)
    diag = jnp.ones((width, 2 * width), f32)
    group = 4
    for first in range(0, width, group):
        across = [
            jnp.broadcast_to(both[:, i : i + 1], both.shape) for i in range(first, first + group)
        ]
        for k in range(group):
            i = first + k
            inv = 1.0 / across[k][i : i + 1, :]
            diag = jnp.where(below == i, inv, diag)
            scaled = both[i : i + 1, :] * inv
            column = jnp.where(below > i, across[k], 0.0)
            for l in range(k + 1, group):
                across[l] = across[l] - column * (across[l][i : i + 1, :] * inv)
            both = both - column * scaled
    inverse = both[:, width:] * jnp.sqrt(diag[:, :width])
    rows = dot3(two(inverse), two(aug[lo : lo + width, :]))
    linv[lo : lo + width, :] = rows[:, n:]
    if lo + width < n:
        start = (lo + width) // 128 * 128
        high, low = two(rows)
        left = (high[:, start:n], low[:, start:n])
        aug[start:, start:] = aug[start:, start:] - dot3(left, (high[:, start:], low[:, start:]), TN)


def kernel(
    nrow, ncol, chunks, skew, width,
    x, pivots, sketch,
    perm_hbm, w_high, w_low, s_high, s_low, upper_out, sketch_out,
    picked, moved_in, from_left, from_right, to_right, to_left,
    panel, perm, product, summed, core_in, reduce_in, totals, gram, gram_in, gram_parts, aug, linv,
    sk_pad, sk_pick, sk_in, sk_part, sk_all,
    zr_s, zr_r, zl_s, zl_r, g1, g2_s, g2_r, g3, c_s, c_r, r_s, r_r, a_s, a_r, f_s, f_r, out_sem,
    gz_s, gz_r, ks_s, ks_r, kz_s, kz_r, ka_s, ka_r, kf_s, kf_r,
):
    rows, columns = x.shape
    n = panel.shape[1]
    tiles = columns // n
    chips = nrow // 2
    share = columns // nrow
    me = lax.axis_index("row")
    z = lax.axis_index("col")
    core = lax.rem(me, 2)
    chip = me // 2
    mate = me + 1 - 2 * core

    def remote(src, dst, ss, rs, dev):
        return pltpu.make_async_remote_copy(
            src_ref=src, dst_ref=dst, send_sem=ss, recv_sem=rs, device_id=dev, device_id_type=MESH
        )

    def peer(d):
        return lax.rem(chip + d, chips) * 2 + core

    def origin(d):
        return lax.rem(chip + chips - d, chips)

    def beside(d):
        return {"row": lax.rem(me + d, nrow)}

    def along(d):
        return {"col": lax.rem(z + d, ncol)}

    barrier = pltpu.get_barrier_semaphore()

    @pl.loop(1, nrow)
    def _(d):
        pl.semaphore_signal(barrier, inc=1, device_id=beside(d), device_id_type=MESH)

    @pl.loop(1, ncol)
    def _(d):
        pl.semaphore_signal(barrier, inc=1, device_id=along(d), device_id_type=MESH)

    def turned(row):
        return jnp.sum(jnp.where(iota((n, n), 0) == iota((n, n), 1), row, 0.0), axis=1, keepdims=True)

    row = pivots[...].astype(f32)
    col = turned(row)
    pos_row = iota((1, n), 1).astype(f32)
    pos_col = iota((n, 1), 0).astype(f32)
    absent_row = 1.0 - jnp.sum(jnp.where(col == pos_row, 1.0, 0.0), axis=0, keepdims=True)
    absent_col = 1.0 - jnp.sum(jnp.where(row == pos_col, 1.0, 0.0), axis=1, keepdims=True)
    rank_col = jnp.sum(jnp.where(pos_row < pos_col, absent_row, 0.0), axis=1, keepdims=True)
    rank_row = jnp.sum(jnp.where((col >= n) & (col < row), 1.0, 0.0), axis=0, keepdims=True)
    taken = jnp.where(rank_col == rank_row, absent_col * pos_col, 0.0)
    partner = jnp.sum(taken, axis=0, keepdims=True)
    piv_col = col.astype(jnp.int32)
    both_col = jnp.concatenate([piv_col, turned(partner).astype(jnp.int32)], axis=0)
    partner = partner.astype(jnp.int32)

    sk, pieces = sketch.shape
    slots = sk_pick.shape[0] // nrow
    spots = iota((1, pieces), 1) + (z * nrow + me) * pieces
    sk_pad[...] = jnp.zeros_like(sk_pad)
    sk_pad[:sk, :] = sketch[...]
    sk_hot = jnp.where(both_col == spots, 1.0, 0.0).astype(bf16)
    k_high, k_mid, k_low = three(sk_pad[...])
    sk_pick[...] = (dot(sk_hot, k_low, NT) + dot(sk_hot, k_mid, NT)) + dot(sk_hot, k_high, NT)

    def slots_of(owner):
        return pl.ds(pl.multiple_of(owner * slots, slots), slots)

    def sk_reduce(d):
        return remote(sk_pick.at[slots_of(lax.rem(me + d, nrow)), :], sk_in.at[d], ks_s.at[d], ks_r.at[d], beside(d))

    def sk_along(d):
        return remote(sk_part.at[0], sk_part.at[d], kz_s.at[d], kz_r.at[d], along(d))

    offset = z * columns
    local = pivots[...] - offset
    mine = (local >= 0) & (local < columns)
    before = local < 0

    pl.semaphore_wait(barrier, nrow + ncol - 2)

    @pl.loop(1, nrow)
    def _(d):
        sk_reduce(d).start()

    former_hot = jnp.where(iota((n, n), 0) == partner, 1.0, 0.0).astype(bf16)
    size = rows // chunks

    picked[...] = jnp.zeros_like(picked)

    @pl.loop(0, tiles)
    def _(t):
        at = pl.multiple_of(t * n, n)
        onehot = jnp.where(iota((n, n), 0) + at == local, 1.0, 0.0).astype(bf16)
        picked[...] += pick3(three(x[:, pl.ds(at, n)]), onehot)

    @pl.when(z == 0)
    def _():
        moved_in[...] = pick3(three(x[:, :n]), former_hot)

    def right(c):
        at = pl.ds(pl.multiple_of(c * size, size), size)
        return remote(to_right.at[at, :], from_left.at[at, :], zr_s.at[c], zr_r.at[c], {"col": z + 1})

    def left(c):
        at = pl.ds(pl.multiple_of(c * size, size), size)
        return remote(to_left.at[at, :], from_right.at[at, :], zl_s.at[c], zl_r.at[c], {"col": z - 1})

    @pl.loop(0, chunks + skew * (ncol - 1))
    def _(t):
        c = t - skew * z

        @pl.when((c >= 0) & (c < chunks))
        def _():
            at = pl.ds(pl.multiple_of(c * size, size), size)

            @pl.when(z > 0)
            def _():
                right(c).wait_recv()
                moved_in[at, :] = from_left[at, :]

            @pl.when(z < ncol - 1)
            def _():
                to_right[at, :] = jnp.where(mine, picked[at, :], moved_in[at, :])
                right(c).start()

        e = t - skew * (ncol - 1 - z)

        @pl.when((e >= 0) & (e < chunks))
        def _():
            at = pl.ds(pl.multiple_of(e * size, size), size)

            @pl.when(z < ncol - 1)
            def _():
                left(e).wait_recv()
                panel[at, :] = jnp.where(mine, picked[at, :], from_right[at, :])

            @pl.when(z == ncol - 1)
            def _():
                panel[at, :] = picked[at, :]

            @pl.when(z > 0)
            def _():
                to_left[at, :] = panel[at, :]
                left(e).start()

    panel[...] = jnp.where(before, moved_in[...], panel[...])

    half = n // 2
    columns_of = panel[...].T
    gram[...] = dot(columns_of, panel[...], precision=highest)
    first = remote(gram, gram_in, g1.at[0], g1.at[1], {"row": mate})
    first.start()

    left_parts = two(columns_of)
    former = three(moved_in[...])
    wanted = piv_col - offset
    usable = piv_col >= n

    first.wait()
    mine_rows = pl.ds(pl.multiple_of(core * half, half), half)
    other_rows = pl.ds(pl.multiple_of((1 - core) * half, half), half)
    quarter = half // ncol

    def gram_rows(place):
        return pl.ds(pl.multiple_of(core * half + place * quarter, quarter), quarter)

    gram_parts[0, :, :] = gram[gram_rows(z), :] + gram_in[gram_rows(z), :]
    aug[:, n:] = jnp.where(iota((n, n), 0) == iota((n, n), 1), 1.0, 0.0).astype(f32)

    def gram_to(d):
        return remote(gram_parts.at[0], gram_parts.at[d], g2_s.at[d], g2_r.at[d], {"row": peer(d)})

    for d in range(1, chips):
        gram_to(d).start()

    def gram_along(d, place):
        at = gram_rows(place)
        return remote(aug.at[at, :n], aug.at[at, :n], gz_s.at[d], gz_r.at[d], along(d))

    last = remote(aug.at[mine_rows, :n], aug.at[mine_rows, :n], g3.at[0], g3.at[1], {"row": mate})

    def gram_over_chips():
        for d in range(1, chips):
            gram_to(d).wait()
        total = jnp.zeros((quarter, n), f32)
        for d in range(chips):
            total = total + gram_parts[lax.rem(chip + chips - d, chips), :, :]
        aug[gram_rows(z), :n] = total
        for d in range(1, ncol):
            gram_along(d, z).start()

    def gram_over_line():
        for d in range(1, ncol):
            gram_along(d, z).wait_send()
            gram_along(d, lax.rem(z + ncol - d, ncol)).wait_recv()
        last.start()

    def out_copy(t):
        at = pl.ds(pl.multiple_of(t * n, n), n)
        return pltpu.make_async_copy(perm.at[:, at], perm_hbm.at[:, at], out_sem.at[t])

    def part(owner):
        return pl.ds(pl.multiple_of(owner * share, share), share)

    def to_mate(c):
        return remote(product.at[part(2 * c + 1 - core), :], core_in.at[c], c_s.at[c], c_r.at[c], {"row": mate})

    def reduce_to(d):
        return remote(totals.at[lax.rem(chip + d, chips)], reduce_in.at[d], r_s.at[d], r_r.at[d], {"row": peer(d)})

    def add_cores(c):
        to_mate(c).wait()
        totals[c, :, :] = product[part(2 * c + core), :] + core_in[c, :, :]

    def send_sums(d):
        add_cores(lax.rem(chip + d, chips))
        reduce_to(d).start()

    per_tile = n // share
    per_chip = 2 * share // n
    begin = lax.rem(chip + 1, chips) * 2 * share // n

    @pl.loop(0, tiles)
    def _(u):
        t = lax.rem(begin + u, tiles)
        at = pl.multiple_of(t * n, n)
        place = (iota((n, n), 1) + at == wanted) & usable
        place = jnp.where(place, 1.0, 0.0)
        keep = 1.0 - jnp.sum(place, axis=0, keepdims=True)
        tile = x[:, pl.ds(at, n)] * keep + pick3(former, place.astype(bf16))
        tile = jnp.where((z == 0) & (t == 0), panel[...], tile)
        perm[:, pl.ds(at, n)] = tile
        out_copy(t).start()
        product[pl.ds(at, n), :] = dot3(left_parts, two(tile)).T

        for i in range(per_tile):
            owner = t * per_tile + i

            @pl.when(lax.rem(owner, 2) != core)
            def _():
                to_mate(owner // 2).start()

        if per_chip > 0:
            ready = (u + 1) // per_chip

            @pl.when((lax.rem(u + 1, per_chip) == 0) & (ready >= 2))
            def _():
                send_sums(ready - 1)

        @pl.when(u == tiles // 2)
        def _():
            gram_over_chips()

        @pl.when(u == tiles - 1)
        def _():
            gram_over_line()

    if per_chip == 0:
        for d in range(1, chips):
            send_sums(d)
    add_cores(chip)

    @pl.loop(1, nrow)
    def _(d):
        sk_reduce(d).wait()

    sk_part[0, :, :] = sk_pick[slots_of(me), :] + jnp.sum(sk_in[1:, :, :], axis=0)
    for d in range(1, ncol):
        sk_along(d).start()

    last.wait_send()
    remote(aug.at[other_rows, :n], aug.at[other_rows, :n], g3.at[0], g3.at[1], {"row": mate}).wait_recv()

    def gather_to(d):
        return remote(summed.at[part(me), :], summed.at[part(me), :], a_s.at[d], a_r.at[d], {"row": peer(d)})

    def gathered(d):
        at = part(origin(d) * 2 + core)
        return remote(summed.at[at, :], summed.at[at, :], a_s.at[d], a_r.at[d], {"row": peer(d)})

    def forward(d):
        at = part(origin(d) * 2 + core)
        return remote(summed.at[at, :], summed.at[at, :], f_s.at[d], f_r.at[d], {"row": mate})

    def forwarded(d):
        at = part(origin(d) * 2 + 1 - core)
        return remote(summed.at[at, :], summed.at[at, :], f_s.at[d], f_r.at[d], {"row": mate})

    def sk_gather_to(d):
        at = slots_of(me)
        return remote(sk_all.at[at, :], sk_all.at[at, :], ka_s.at[d], ka_r.at[d], {"row": peer(d)})

    def sk_gathered(d):
        at = slots_of(origin(d) * 2 + core)
        return remote(sk_all.at[at, :], sk_all.at[at, :], ka_s.at[d], ka_r.at[d], {"row": peer(d)})

    def sk_forward(d):
        at = slots_of(origin(d) * 2 + core)
        return remote(sk_all.at[at, :], sk_all.at[at, :], kf_s.at[d], kf_r.at[d], {"row": mate})

    def sk_forwarded(d):
        at = slots_of(origin(d) * 2 + 1 - core)
        return remote(sk_all.at[at, :], sk_all.at[at, :], kf_s.at[d], kf_r.at[d], {"row": mate})

    def finish_reduce():
        total = totals[chip, :, :]
        for d in range(1, chips):
            reduce_to(d).wait()
            total = total + reduce_in[d, :, :]
        summed[part(me), :] = total
        for d in range(1, chips):
            gather_to(d).start()
        forward(0).start()
        for d in range(1, ncol):
            sk_along(d).wait()
        sk_all[slots_of(me), :] = jnp.sum(sk_part[...], axis=0)
        for d in range(1, chips):
            sk_gather_to(d).start()
        sk_forward(0).start()

    def finish_gather():
        for d in range(1, chips):
            gathered(d).wait_recv()
            forward(d).start()

    blocks = n // width
    for b in range(blocks):
        cholesky_block(aug, linv, b, width)
        if b == blocks // 2 - 1:
            finish_reduce()
    finish_gather()
    for d in range(1, chips):
        sk_gathered(d).wait_recv()
        sk_forward(d).start()

    inverse = dot3(two(linv[...]), two(linv[...]), TN)
    w_high[...], w_low[...] = two(dot3(two(panel[...]), two(inverse)))
    own = two(summed[part(me), :])
    upper_out[...] = dot3(two(linv[...]), own, NT)
    solved = dot3(two(inverse), own, NT)

    for d in range(chips):
        forwarded(d).wait_recv()

    @pl.loop(0, tiles)
    def _(t):
        at = pl.ds(pl.multiple_of(t * n, n), n)
        high, low = two(summed[at, :].T)
        s_high[:, at] = high
        s_low[:, at] = low

    for d in range(chips):
        sk_forwarded(d).wait_recv()
    into = jnp.where((spots == piv_col) & (piv_col >= n), 1.0, 0.0)
    leading = jnp.where(spots == iota((n, 1), 0), 1.0, 0.0)
    chosen = jnp.concatenate([leading, into], axis=0)
    stay = 1.0 - jnp.sum(chosen, axis=0, keepdims=True)
    turned_all = sk_all[...].T
    changed = pick3(three(turned_all), chosen.astype(bf16)) - dot3(two(turned_all[:, :n]), two(solved))
    sketch_out[...] = sketch[...] * stay + changed[:sk, :]

    for d in range(1, chips):
        gather_to(d).wait_send()
        sk_gather_to(d).wait_send()
    for d in range(chips):
        forward(d).wait_send()
        sk_forward(d).wait_send()

    @pl.loop(0, chunks)
    def _(c):
        @pl.when(z < ncol - 1)
        def _():
            right(c).wait_send()

        @pl.when(z > 0)
        def _():
            left(c).wait_send()

    @pl.loop(0, tiles)
    def _(t):
        out_copy(t).wait()


def project(perm, w_high, w_low, s_high, s_low, upper, sketch, out, upper_out, sketch_out):
    @pl.when(pl.program_id(0) == 0)
    def _():
        upper_out[...] = upper[...]
        sketch_out[...] = sketch[...]

    out[...] = perm[...] - dot3((w_high[...], w_low[...]), (s_high[...], s_low[...]))


def per_device(nrow, ncol, matrix, pivots, sketch):
    rows, columns = matrix.shape
    n = pivots.shape[0]
    sk, pieces = sketch.shape
    padded = (sk + 127) // 128 * 128
    chunks = 20
    skew = 3
    width = 64
    chips = nrow // 2
    share = columns // nrow
    slots = 2 * n // nrow
    vmem = pl.BlockSpec(memory_space=pltpu.VMEM)
    full = pltpu.VMEM((rows, n), f32)
    dma = pltpu.SemaphoreType.DMA
    shape = jax.ShapeDtypeStruct
    perm, w_high, w_low, s_high, s_low, upper, new_sketch = pl.pallas_call(
        functools.partial(kernel, nrow, ncol, chunks, skew, width),
        out_shape=[
            shape((rows, columns), f32),
            shape((rows, n), bf16),
            shape((rows, n), bf16),
            shape((n, columns), bf16),
            shape((n, columns), bf16),
            shape((n, share), f32),
            shape((sk, pieces), f32),
        ],
        in_specs=[vmem] * 3,
        out_specs=[pl.BlockSpec(memory_space=pl.ANY)] + [vmem] * 6,
        scratch_shapes=[
            full, full, full, full, full, full, full,
            pltpu.VMEM((rows, columns), f32),
            pltpu.VMEM((columns, n), f32),
            pltpu.VMEM((columns, n), f32),
            pltpu.VMEM((chips, share, n), f32),
            pltpu.VMEM((chips, share, n), f32),
            pltpu.VMEM((chips, share, n), f32),
            pltpu.VMEM((n, n), f32),
            pltpu.VMEM((n, n), f32),
            pltpu.VMEM((chips, n // 2 // ncol, n), f32),
            pltpu.VMEM((n, 2 * n), f32),
            pltpu.VMEM((n, n), f32),
            pltpu.VMEM((padded, pieces), f32),
            pltpu.VMEM((2 * n, padded), f32),
            pltpu.VMEM((nrow, slots, padded), f32),
            pltpu.VMEM((ncol, slots, padded), f32),
            pltpu.VMEM((2 * n, padded), f32),
            dma((chunks,)), dma((chunks,)), dma((chunks,)), dma((chunks,)),
            dma((2,)), dma((chips,)), dma((chips,)), dma((2,)),
            dma((chips,)), dma((chips,)), dma((chips,)), dma((chips,)),
            dma((chips,)), dma((chips,)), dma((chips,)), dma((chips,)),
            dma((columns // n,)),
            dma((ncol,)), dma((ncol,)),
            dma((nrow,)), dma((nrow,)), dma((ncol,)), dma((ncol,)),
            dma((chips,)), dma((chips,)), dma((chips,)), dma((chips,)),
        ],
        compiler_params=pltpu.CompilerParams(
            collective_id=0, has_side_effects=True, vmem_limit_bytes=56 * 1024 * 1024
        ),
        cost_estimate=pl.CostEstimate(
            flops=20 * rows * n * columns, bytes_accessed=8 * rows * columns, transcendentals=0
        ),
    )(matrix, pivots[None, :], sketch)

    tile = 2 * n
    whole = pl.BlockSpec((rows, n), lambda i: (0, 0))
    across = pl.BlockSpec((n, tile), lambda i: (0, i))
    small = [pl.BlockSpec(a.shape, lambda i: (0, 0)) for a in (upper, new_sketch)]
    trailing, upper, new_sketch = pl.pallas_call(
        project,
        grid=(columns // tile,),
        out_shape=[shape((rows, columns), f32), shape(upper.shape, f32), shape(new_sketch.shape, f32)],
        in_specs=[pl.BlockSpec((rows, tile), lambda i: (0, i)), whole, whole, across, across]
        + small,
        out_specs=[pl.BlockSpec((rows, tile), lambda i: (0, i))] + small,
        compiler_params=pltpu.CompilerParams(vmem_limit_bytes=56 * 1024 * 1024),
    )(perm, w_high, w_low, s_high, s_low, upper, new_sketch)
    return (upper, trailing, new_sketch)


def solution(mesh):
    return jax.shard_map(
        functools.partial(per_device, mesh.shape["row"], mesh.shape["col"]),
        mesh=mesh,
        in_specs=(P("row", "col"), P(), P(None, ("col", "row"))),
        out_specs=(P(None, ("col", "row")), P("row", "col"), P(None, ("col", "row"))),
        check_vma=False,
    )
```

```python
import functools

import jax
import jax.numpy as jnp
from jax import lax
from jax.experimental import pallas as pl
from jax.experimental.pallas import tpu as pltpu
from jax.sharding import PartitionSpec as P

highest = lax.Precision.HIGHEST
f32 = jnp.float32
bf16 = jnp.bfloat16
MESH = pl.DeviceIdType.MESH
NN = (((1,), (0,)), ((), ()))
NT = (((1,), (1,)), ((), ()))
TN = (((0,), (0,)), ((), ()))


def dot(a, b, dims=NN, precision=None):
    return lax.dot_general(a, b, dims, precision=precision, preferred_element_type=f32)


def two(x):
    high = x.astype(bf16)
    return high, (x - high.astype(f32)).astype(bf16)


def three(x):
    high = x.astype(bf16)
    rest = x - high.astype(f32)
    mid = rest.astype(bf16)
    return high, mid, (rest - mid.astype(f32)).astype(bf16)


def dot3(a, b, dims=NN):
    (ah, al), (bh, bl) = a, b
    ((i,), (j,)), _ = dims
    if ah.shape[i] % 64 == 0:
        left = jnp.concatenate([al, ah, ah], axis=i)
        return dot(left, jnp.concatenate([bh, bl, bh], axis=j), dims)
    return dot(ah, bh, dims) + (dot(ah, bl, dims) + dot(al, bh, dims))


def pick3(parts, onehot):
    high, mid, low = parts
    left = jnp.concatenate([low, mid, high], axis=1)
    return dot(left, jnp.concatenate([onehot] * 3, axis=0))


def iota(shape, axis):
    return lax.broadcasted_iota(jnp.int32, shape, axis)


def cholesky_block(aug, linv, b, width):
    n = aug.shape[0]
    lo = b * width
    eye = jnp.where(iota((width, width), 0) == iota((width, width), 1), 1.0, 0.0).astype(f32)
    both = jnp.concatenate([aug[lo : lo + width, lo : lo + width], eye], axis=1)
    below = iota((width, 2 * width), 0)
    diag = jnp.ones((width, 2 * width), f32)
    group = 4
    for first in range(0, width, group):
        across = [
            jnp.broadcast_to(both[:, i : i + 1], both.shape) for i in range(first, first + group)
        ]
        for k in range(group):
            i = first + k
            inv = 1.0 / across[k][i : i + 1, :]
            diag = jnp.where(below == i, inv, diag)
            scaled = both[i : i + 1, :] * inv
            column = jnp.where(below > i, across[k], 0.0)
            for l in range(k + 1, group):
                across[l] = across[l] - column * (across[l][i : i + 1, :] * inv)
            both = both - column * scaled
    inverse = both[:, width:] * jnp.sqrt(diag[:, :width])
    rows = dot3(two(inverse), two(aug[lo : lo + width, :]))
    linv[lo : lo + width, :] = rows[:, n:]
    if lo + width < n:
        start = (lo + width) // 128 * 128
        high, low = two(rows)
        left = (high[:, start:n], low[:, start:n])
        aug[start:, start:] = aug[start:, start:] - dot3(left, (high[:, start:], low[:, start:]), TN)


def kernel(
    nrow, ncol, chunks, skew, width,
    x, pivots, sketch,
    perm_hbm, w_high, w_low, s_high, s_low, upper_out, sketch_out,
    picked, moved_in, from_left, from_right, to_right, to_left,
    panel, perm, product, summed, core_in, reduce_in, totals, gram, gram_in, gram_parts, aug, linv,
    sk_pad, sk_pick, sk_in, sk_part, sk_all,
    zr_s, zr_r, zl_s, zl_r, g1, g2_s, g2_r, g3, c_s, c_r, r_s, r_r, a_s, a_r, f_s, f_r, out_sem,
    gz_s, gz_r, ks_s, ks_r, kz_s, kz_r, ka_s, ka_r, kf_s, kf_r,
):
    rows, columns = x.shape
    n = panel.shape[1]
    tiles = columns // n
    chips = nrow // 2
    share = columns // nrow
    me = lax.axis_index("row")
    z = lax.axis_index("col")
    core = lax.rem(me, 2)
    chip = me // 2
    mate = me + 1 - 2 * core

    def remote(src, dst, ss, rs, dev):
        return pltpu.make_async_remote_copy(
            src_ref=src, dst_ref=dst, send_sem=ss, recv_sem=rs, device_id=dev, device_id_type=MESH
        )

    def peer(d):
        return lax.rem(chip + d, chips) * 2 + core

    def origin(d):
        return lax.rem(chip + chips - d, chips)

    def beside(d):
        return {"row": lax.rem(me + d, nrow)}

    def along(d):
        return {"col": lax.rem(z + d, ncol)}

    barrier = pltpu.get_barrier_semaphore()

    @pl.loop(1, nrow)
    def _(d):
        pl.semaphore_signal(barrier, inc=1, device_id=beside(d), device_id_type=MESH)

    @pl.loop(1, ncol)
    def _(d):
        pl.semaphore_signal(barrier, inc=1, device_id=along(d), device_id_type=MESH)

    def turned(row):
        return jnp.sum(jnp.where(iota((n, n), 0) == iota((n, n), 1), row, 0.0), axis=1, keepdims=True)

    row = pivots[...].astype(f32)
    col = turned(row)
    pos_row = iota((1, n), 1).astype(f32)
    pos_col = iota((n, 1), 0).astype(f32)
    absent_row = 1.0 - jnp.sum(jnp.where(col == pos_row, 1.0, 0.0), axis=0, keepdims=True)
    absent_col = 1.0 - jnp.sum(jnp.where(row == pos_col, 1.0, 0.0), axis=1, keepdims=True)
    rank_col = jnp.sum(jnp.where(pos_row < pos_col, absent_row, 0.0), axis=1, keepdims=True)
    rank_row = jnp.sum(jnp.where((col >= n) & (col < row), 1.0, 0.0), axis=0, keepdims=True)
    taken = jnp.where(rank_col == rank_row, absent_col * pos_col, 0.0)
    partner = jnp.sum(taken, axis=0, keepdims=True)
    piv_col = col.astype(jnp.int32)
    both_col = jnp.concatenate([piv_col, turned(partner).astype(jnp.int32)], axis=0)
    partner = partner.astype(jnp.int32)

    sk, pieces = sketch.shape
    slots = sk_pick.shape[0] // nrow
    spots = iota((1, pieces), 1) + (z * nrow + me) * pieces
    sk_pad[...] = jnp.zeros_like(sk_pad)
    sk_pad[:sk, :] = sketch[...]
    sk_hot = jnp.where(both_col == spots, 1.0, 0.0).astype(bf16)
    k_high, k_mid, k_low = three(sk_pad[...])
    sk_pick[...] = (dot(sk_hot, k_low, NT) + dot(sk_hot, k_mid, NT)) + dot(sk_hot, k_high, NT)

    def slots_of(owner):
        return pl.ds(pl.multiple_of(owner * slots, slots), slots)

    def sk_reduce(d):
        return remote(sk_pick.at[slots_of(lax.rem(me + d, nrow)), :], sk_in.at[d], ks_s.at[d], ks_r.at[d], beside(d))

    def sk_along(d):
        return remote(sk_part.at[0], sk_part.at[d], kz_s.at[d], kz_r.at[d], along(d))

    offset = z * columns
    local = pivots[...] - offset
    mine = (local >= 0) & (local < columns)
    before = local < 0

    pl.semaphore_wait(barrier, nrow + ncol - 2)

    @pl.loop(1, nrow)
    def _(d):
        sk_reduce(d).start()

    former_hot = jnp.where(iota((n, n), 0) == partner, 1.0, 0.0).astype(bf16)
    size = rows // chunks

    picked[...] = jnp.zeros_like(picked)

    @pl.loop(0, tiles)
    def _(t):
        at = pl.multiple_of(t * n, n)
        onehot = jnp.where(iota((n, n), 0) + at == local, 1.0, 0.0).astype(bf16)
        picked[...] += pick3(three(x[:, pl.ds(at, n)]), onehot)

    @pl.when(z == 0)
    def _():
        moved_in[...] = pick3(three(x[:, :n]), former_hot)

    def right(c):
        at = pl.ds(pl.multiple_of(c * size, size), size)
        return remote(to_right.at[at, :], from_left.at[at, :], zr_s.at[c], zr_r.at[c], {"col": z + 1})

    def left(c):
        at = pl.ds(pl.multiple_of(c * size, size), size)
        return remote(to_left.at[at, :], from_right.at[at, :], zl_s.at[c], zl_r.at[c], {"col": z - 1})

    @pl.loop(0, chunks + skew * (ncol - 1))
    def _(t):
        c = t - skew * z

        @pl.when((c >= 0) & (c < chunks))
        def _():
            at = pl.ds(pl.multiple_of(c * size, size), size)

            @pl.when(z > 0)
            def _():
                right(c).wait_recv()
                moved_in[at, :] = from_left[at, :]

            @pl.when(z < ncol - 1)
            def _():
                to_right[at, :] = jnp.where(mine, picked[at, :], moved_in[at, :])
                right(c).start()

        e = t - skew * (ncol - 1 - z)

        @pl.when((e >= 0) & (e < chunks))
        def _():
            at = pl.ds(pl.multiple_of(e * size, size), size)

            @pl.when(z < ncol - 1)
            def _():
                left(e).wait_recv()
                panel[at, :] = jnp.where(mine, picked[at, :], from_right[at, :])

            @pl.when(z == ncol - 1)
            def _():
                panel[at, :] = picked[at, :]

            @pl.when(z > 0)
            def _():
                to_left[at, :] = panel[at, :]
                left(e).start()

    panel[...] = jnp.where(before, moved_in[...], panel[...])

    half = n // 2
    columns_of = panel[...].T
    gram[...] = dot(columns_of, panel[...], precision=highest)
    first = remote(gram, gram_in, g1.at[0], g1.at[1], {"row": mate})
    first.start()

    left_parts = two(columns_of)
    former = three(moved_in[...])
    wanted = piv_col - offset
    usable = piv_col >= n

    first.wait()
    mine_rows = pl.ds(pl.multiple_of(core * half, half), half)
    other_rows = pl.ds(pl.multiple_of((1 - core) * half, half), half)
    quarter = half // ncol

    def gram_rows(place):
        return pl.ds(pl.multiple_of(core * half + place * quarter, quarter), quarter)

    gram_parts[0, :, :] = gram[gram_rows(z), :] + gram_in[gram_rows(z), :]
    aug[:, n:] = jnp.where(iota((n, n), 0) == iota((n, n), 1), 1.0, 0.0).astype(f32)

    def gram_to(d):
        return remote(gram_parts.at[0], gram_parts.at[d], g2_s.at[d], g2_r.at[d], {"row": peer(d)})

    for d in range(1, chips):
        gram_to(d).start()

    def gram_along(d, place):
        at = gram_rows(place)
        return remote(aug.at[at, :n], aug.at[at, :n], gz_s.at[d], gz_r.at[d], along(d))

    last = remote(aug.at[mine_rows, :n], aug.at[mine_rows, :n], g3.at[0], g3.at[1], {"row": mate})

    def gram_over_chips():
        for d in range(1, chips):
            gram_to(d).wait()
        total = jnp.zeros((quarter, n), f32)
        for d in range(chips):
            total = total + gram_parts[lax.rem(chip + chips - d, chips), :, :]
        aug[gram_rows(z), :n] = total
        for d in range(1, ncol):
            gram_along(d, z).start()

    def gram_over_line():
        for d in range(1, ncol):
            gram_along(d, z).wait_send()
            gram_along(d, lax.rem(z + ncol - d, ncol)).wait_recv()
        last.start()

    def out_copy(t):
        at = pl.ds(pl.multiple_of(t * n, n), n)
        return pltpu.make_async_copy(perm.at[:, at], perm_hbm.at[:, at], out_sem.at[t])

    def part(owner):
        return pl.ds(pl.multiple_of(owner * share, share), share)

    def to_mate(c):
        return remote(product.at[part(2 * c + 1 - core), :], core_in.at[c], c_s.at[c], c_r.at[c], {"row": mate})

    def reduce_to(d):
        return remote(totals.at[lax.rem(chip + d, chips)], reduce_in.at[d], r_s.at[d], r_r.at[d], {"row": peer(d)})

    def add_cores(c):
        to_mate(c).wait()
        totals[c, :, :] = product[part(2 * c + core), :] + core_in[c, :, :]

    def send_sums(d):
        add_cores(lax.rem(chip + d, chips))
        reduce_to(d).start()

    per_tile = n // share
    per_chip = 2 * share // n
    begin = lax.rem(chip + 1, chips) * 2 * share // n

    @pl.loop(0, tiles)
    def _(u):
        t = lax.rem(begin + u, tiles)
        at = pl.multiple_of(t * n, n)
        place = (iota((n, n), 1) + at == wanted) & usable
        place = jnp.where(place, 1.0, 0.0)
        keep = 1.0 - jnp.sum(place, axis=0, keepdims=True)
        tile = x[:, pl.ds(at, n)] * keep + pick3(former, place.astype(bf16))
        tile = jnp.where((z == 0) & (t == 0), panel[...], tile)
        perm[:, pl.ds(at, n)] = tile
        out_copy(t).start()
        product[pl.ds(at, n), :] = dot3(left_parts, two(tile)).T

        for i in range(per_tile):
            owner = t * per_tile + i

            @pl.when(lax.rem(owner, 2) != core)
            def _():
                to_mate(owner // 2).start()

        if per_chip > 0:
            ready = (u + 1) // per_chip

            @pl.when((lax.rem(u + 1, per_chip) == 0) & (ready >= 2))
            def _():
                send_sums(ready - 1)

        @pl.when(u == tiles // 2)
        def _():
            gram_over_chips()

        @pl.when(u == tiles - 1)
        def _():
            gram_over_line()

    if per_chip == 0:
        for d in range(1, chips):
            send_sums(d)
    add_cores(chip)

    @pl.loop(1, nrow)
    def _(d):
        sk_reduce(d).wait()

    sk_part[0, :, :] = sk_pick[slots_of(me), :] + jnp.sum(sk_in[1:, :, :], axis=0)
    for d in range(1, ncol):
        sk_along(d).start()

    last.wait_send()
    remote(aug.at[other_rows, :n], aug.at[other_rows, :n], g3.at[0], g3.at[1], {"row": mate}).wait_recv()

    def gather_to(d):
        return remote(summed.at[part(me), :], summed.at[part(me), :], a_s.at[d], a_r.at[d], {"row": peer(d)})

    def gathered(d):
        at = part(origin(d) * 2 + core)
        return remote(summed.at[at, :], summed.at[at, :], a_s.at[d], a_r.at[d], {"row": peer(d)})

    def forward(d):
        at = part(origin(d) * 2 + core)
        return remote(summed.at[at, :], summed.at[at, :], f_s.at[d], f_r.at[d], {"row": mate})

    def forwarded(d):
        at = part(origin(d) * 2 + 1 - core)
        return remote(summed.at[at, :], summed.at[at, :], f_s.at[d], f_r.at[d], {"row": mate})

    def sk_gather_to(d):
        at = slots_of(me)
        return remote(sk_all.at[at, :], sk_all.at[at, :], ka_s.at[d], ka_r.at[d], {"row": peer(d)})

    def sk_gathered(d):
        at = slots_of(origin(d) * 2 + core)
        return remote(sk_all.at[at, :], sk_all.at[at, :], ka_s.at[d], ka_r.at[d], {"row": peer(d)})

    def sk_forward(d):
        at = slots_of(origin(d) * 2 + core)
        return remote(sk_all.at[at, :], sk_all.at[at, :], kf_s.at[d], kf_r.at[d], {"row": mate})

    def sk_forwarded(d):
        at = slots_of(origin(d) * 2 + 1 - core)
        return remote(sk_all.at[at, :], sk_all.at[at, :], kf_s.at[d], kf_r.at[d], {"row": mate})

    def finish_reduce():
        total = totals[chip, :, :]
        for d in range(1, chips):
            reduce_to(d).wait()
            total = total + reduce_in[d, :, :]
        summed[part(me), :] = total
        for d in range(1, chips):
            gather_to(d).start()
        forward(0).start()

    def finish_sketch():
        for d in range(1, ncol):
            sk_along(d).wait()
        sk_all[slots_of(me), :] = jnp.sum(sk_part[...], axis=0)
        for d in range(1, chips):
            sk_gather_to(d).start()
        sk_forward(0).start()

    def finish_gather():
        for d in range(1, chips):
            gathered(d).wait_recv()
            forward(d).start()

    blocks = n // width
    for b in range(blocks):
        cholesky_block(aug, linv, b, width)
        if b == 0:
            finish_reduce()
        if b == blocks // 2 - 1:
            finish_sketch()
    finish_gather()
    for d in range(1, chips):
        sk_gathered(d).wait_recv()
        sk_forward(d).start()

    inverse = dot3(two(linv[...]), two(linv[...]), TN)
    w_high[...], w_low[...] = two(dot3(two(panel[...]), two(inverse)))
    own = two(summed[part(me), :])
    upper_out[...] = dot3(two(linv[...]), own, NT)
    solved = dot3(two(inverse), own, NT)

    for d in range(chips):
        forwarded(d).wait_recv()

    @pl.loop(0, tiles)
    def _(t):
        at = pl.ds(pl.multiple_of(t * n, n), n)
        high, low = two(summed[at, :].T)
        s_high[:, at] = high
        s_low[:, at] = low

    for d in range(chips):
        sk_forwarded(d).wait_recv()
    into = jnp.where((spots == piv_col) & (piv_col >= n), 1.0, 0.0)
    leading = jnp.where(spots == iota((n, 1), 0), 1.0, 0.0)
    chosen = jnp.concatenate([leading, into], axis=0)
    stay = 1.0 - jnp.sum(chosen, axis=0, keepdims=True)
    turned_all = sk_all[...].T
    changed = pick3(three(turned_all), chosen.astype(bf16)) - dot3(two(turned_all[:, :n]), two(solved))
    sketch_out[...] = sketch[...] * stay + changed[:sk, :]

    for d in range(1, chips):
        gather_to(d).wait_send()
        sk_gather_to(d).wait_send()
    for d in range(chips):
        forward(d).wait_send()
        sk_forward(d).wait_send()

    @pl.loop(0, chunks)
    def _(c):
        @pl.when(z < ncol - 1)
        def _():
            right(c).wait_send()

        @pl.when(z > 0)
        def _():
            left(c).wait_send()

    @pl.loop(0, tiles)
    def _(t):
        out_copy(t).wait()


def project(perm, w_high, w_low, s_high, s_low, upper, sketch, out, upper_out, sketch_out):
    @pl.when(pl.program_id(0) == 0)
    def _():
        upper_out[...] = upper[...]
        sketch_out[...] = sketch[...]

    out[...] = perm[...] - dot3((w_high[...], w_low[...]), (s_high[...], s_low[...]))


def per_device(nrow, ncol, matrix, pivots, sketch):
    rows, columns = matrix.shape
    n = pivots.shape[0]
    sk, pieces = sketch.shape
    padded = (sk + 127) // 128 * 128
    chunks = 20
    skew = 3
    width = 64
    chips = nrow // 2
    share = columns // nrow
    slots = 2 * n // nrow
    vmem = pl.BlockSpec(memory_space=pltpu.VMEM)
    full = pltpu.VMEM((rows, n), f32)
    dma = pltpu.SemaphoreType.DMA
    shape = jax.ShapeDtypeStruct
    perm, w_high, w_low, s_high, s_low, upper, new_sketch = pl.pallas_call(
        functools.partial(kernel, nrow, ncol, chunks, skew, width),
        out_shape=[
            shape((rows, columns), f32),
            shape((rows, n), bf16),
            shape((rows, n), bf16),
            shape((n, columns), bf16),
            shape((n, columns), bf16),
            shape((n, share), f32),
            shape((sk, pieces), f32),
        ],
        in_specs=[vmem] * 3,
        out_specs=[pl.BlockSpec(memory_space=pl.ANY)] + [vmem] * 6,
        scratch_shapes=[
            full, full, full, full, full, full, full,
            pltpu.VMEM((rows, columns), f32),
            pltpu.VMEM((columns, n), f32),
            pltpu.VMEM((columns, n), f32),
            pltpu.VMEM((chips, share, n), f32),
            pltpu.VMEM((chips, share, n), f32),
            pltpu.VMEM((chips, share, n), f32),
            pltpu.VMEM((n, n), f32),
            pltpu.VMEM((n, n), f32),
            pltpu.VMEM((chips, n // 2 // ncol, n), f32),
            pltpu.VMEM((n, 2 * n), f32),
            pltpu.VMEM((n, n), f32),
            pltpu.VMEM((padded, pieces), f32),
            pltpu.VMEM((2 * n, padded), f32),
            pltpu.VMEM((nrow, slots, padded), f32),
            pltpu.VMEM((ncol, slots, padded), f32),
            pltpu.VMEM((2 * n, padded), f32),
            dma((chunks,)), dma((chunks,)), dma((chunks,)), dma((chunks,)),
            dma((2,)), dma((chips,)), dma((chips,)), dma((2,)),
            dma((chips,)), dma((chips,)), dma((chips,)), dma((chips,)),
            dma((chips,)), dma((chips,)), dma((chips,)), dma((chips,)),
            dma((columns // n,)),
            dma((ncol,)), dma((ncol,)),
            dma((nrow,)), dma((nrow,)), dma((ncol,)), dma((ncol,)),
            dma((chips,)), dma((chips,)), dma((chips,)), dma((chips,)),
        ],
        compiler_params=pltpu.CompilerParams(
            collective_id=0, has_side_effects=True, vmem_limit_bytes=56 * 1024 * 1024
        ),
        cost_estimate=pl.CostEstimate(
            flops=20 * rows * n * columns, bytes_accessed=8 * rows * columns, transcendentals=0
        ),
    )(matrix, pivots[None, :], sketch)

    tile = 2 * n
    whole = pl.BlockSpec((rows, n), lambda i: (0, 0))
    across = pl.BlockSpec((n, tile), lambda i: (0, i))
    small = [pl.BlockSpec(a.shape, lambda i: (0, 0)) for a in (upper, new_sketch)]
    trailing, upper, new_sketch = pl.pallas_call(
        project,
        grid=(columns // tile,),
        out_shape=[shape((rows, columns), f32), shape(upper.shape, f32), shape(new_sketch.shape, f32)],
        in_specs=[pl.BlockSpec((rows, tile), lambda i: (0, i)), whole, whole, across, across]
        + small,
        out_specs=[pl.BlockSpec((rows, tile), lambda i: (0, i))] + small,
        compiler_params=pltpu.CompilerParams(vmem_limit_bytes=56 * 1024 * 1024),
    )(perm, w_high, w_low, s_high, s_low, upper, new_sketch)
    return (upper, trailing, new_sketch)


def solution(mesh):
    return jax.shard_map(
        functools.partial(per_device, mesh.shape["row"], mesh.shape["col"]),
        mesh=mesh,
        in_specs=(P("row", "col"), P(), P(None, ("col", "row"))),
        out_specs=(P(None, ("col", "row")), P("row", "col"), P(None, ("col", "row"))),
        check_vma=False,
    )
```

```python
import functools

import jax
import jax.numpy as jnp
from jax import lax
from jax.experimental import pallas as pl
from jax.experimental.pallas import tpu as pltpu
from jax.sharding import PartitionSpec as P

highest = lax.Precision.HIGHEST
f32 = jnp.float32
bf16 = jnp.bfloat16
MESH = pl.DeviceIdType.MESH
NN = (((1,), (0,)), ((), ()))
NT = (((1,), (1,)), ((), ()))
TN = (((0,), (0,)), ((), ()))


def dot(a, b, dims=NN, precision=None):
    return lax.dot_general(a, b, dims, precision=precision, preferred_element_type=f32)


def two(x):
    high = x.astype(bf16)
    return high, (x - high.astype(f32)).astype(bf16)


def three(x):
    high = x.astype(bf16)
    rest = x - high.astype(f32)
    mid = rest.astype(bf16)
    return high, mid, (rest - mid.astype(f32)).astype(bf16)


def dot3(a, b, dims=NN):
    (ah, al), (bh, bl) = a, b
    ((i,), (j,)), _ = dims
    if ah.shape[i] % 64 == 0:
        left = jnp.concatenate([al, ah, ah], axis=i)
        return dot(left, jnp.concatenate([bh, bl, bh], axis=j), dims)
    return dot(ah, bh, dims) + (dot(ah, bl, dims) + dot(al, bh, dims))


def pick3(parts, onehot):
    high, mid, low = parts
    left = jnp.concatenate([low, mid, high], axis=1)
    return dot(left, jnp.concatenate([onehot] * 3, axis=0))


def iota(shape, axis):
    return lax.broadcasted_iota(jnp.int32, shape, axis)


def cholesky_block(aug, linv, b, width):
    n = aug.shape[0]
    lo = b * width
    eye = jnp.where(iota((width, width), 0) == iota((width, width), 1), 1.0, 0.0).astype(f32)
    both = jnp.concatenate([aug[lo : lo + width, lo : lo + width], eye], axis=1)
    group = 8
    done, scales = [], []
    for first in range(0, width, group):
        below = iota(both.shape, 0)
        across = [
            jnp.broadcast_to(both[:, i : i + 1], both.shape) for i in range(first, first + group)
        ]
        scale = jnp.ones((group, 2 * width), f32)
        for k in range(group):
            inv = 1.0 / across[k][k : k + 1, :]
            scale = jnp.where(below[:group, :] == k, inv, scale)
            scaled = both[k : k + 1, :] * inv
            column = jnp.where(below > k, across[k], 0.0)
            for l in range(k + 1, group):
                across[l] = across[l] - column * (across[l][k : k + 1, :] * inv)
            both = both - column * scaled
        done.append(both[:group, :])
        scales.append(scale)
        both = both[group:, :]
    both = jnp.concatenate(done, axis=0)
    diag = jnp.concatenate(scales, axis=0)
    inverse = both[:, width:] * jnp.sqrt(diag[:, :width])
    rows = dot3(two(inverse), two(aug[lo : lo + width, :]))
    linv[lo : lo + width, :] = rows[:, n:]
    if lo + width < n:
        start = (lo + width) // 128 * 128
        high, low = two(rows)
        left = (high[:, start:n], low[:, start:n])
        aug[start:, start:] = aug[start:, start:] - dot3(left, (high[:, start:], low[:, start:]), TN)


def kernel(
    nrow, ncol, chunks, skew, width,
    x, pivots, sketch,
    perm_hbm, w_high, w_low, s_high, s_low, upper_out, sketch_out,
    picked, moved_in, from_left, from_right, to_right, to_left,
    panel, perm, product, summed, core_in, reduce_in, totals, gram, gram_in, gram_parts, aug, linv,
    sk_pad, sk_pick, sk_in, sk_part, sk_all,
    zr_s, zr_r, zl_s, zl_r, g1, g2_s, g2_r, g3, c_s, c_r, r_s, r_r, a_s, a_r, f_s, f_r, out_sem,
    gz_s, gz_r, ks_s, ks_r, kz_s, kz_r, ka_s, ka_r, kf_s, kf_r,
):
    rows, columns = x.shape
    n = panel.shape[1]
    tiles = columns // n
    chips = nrow // 2
    share = columns // nrow
    me = lax.axis_index("row")
    z = lax.axis_index("col")
    core = lax.rem(me, 2)
    chip = me // 2
    mate = me + 1 - 2 * core

    def remote(src, dst, ss, rs, dev):
        return pltpu.make_async_remote_copy(
            src_ref=src, dst_ref=dst, send_sem=ss, recv_sem=rs, device_id=dev, device_id_type=MESH
        )

    def peer(d):
        return lax.rem(chip + d, chips) * 2 + core

    def origin(d):
        return lax.rem(chip + chips - d, chips)

    def beside(d):
        return {"row": lax.rem(me + d, nrow)}

    def along(d):
        return {"col": lax.rem(z + d, ncol)}

    barrier = pltpu.get_barrier_semaphore()

    @pl.loop(1, nrow)
    def _(d):
        pl.semaphore_signal(barrier, inc=1, device_id=beside(d), device_id_type=MESH)

    @pl.loop(1, ncol)
    def _(d):
        pl.semaphore_signal(barrier, inc=1, device_id=along(d), device_id_type=MESH)

    def turned(row):
        return jnp.sum(jnp.where(iota((n, n), 0) == iota((n, n), 1), row, 0.0), axis=1, keepdims=True)

    row = pivots[...].astype(f32)
    col = turned(row)
    pos_row = iota((1, n), 1).astype(f32)
    pos_col = iota((n, 1), 0).astype(f32)
    absent_row = 1.0 - jnp.sum(jnp.where(col == pos_row, 1.0, 0.0), axis=0, keepdims=True)
    absent_col = 1.0 - jnp.sum(jnp.where(row == pos_col, 1.0, 0.0), axis=1, keepdims=True)
    rank_col = jnp.sum(jnp.where(pos_row < pos_col, absent_row, 0.0), axis=1, keepdims=True)
    rank_row = jnp.sum(jnp.where((col >= n) & (col < row), 1.0, 0.0), axis=0, keepdims=True)
    taken = jnp.where(rank_col == rank_row, absent_col * pos_col, 0.0)
    partner = jnp.sum(taken, axis=0, keepdims=True)
    piv_col = col.astype(jnp.int32)
    both_col = jnp.concatenate([piv_col, turned(partner).astype(jnp.int32)], axis=0)
    partner = partner.astype(jnp.int32)

    sk, pieces = sketch.shape
    slots = sk_pick.shape[0] // nrow
    spots = iota((1, pieces), 1) + (z * nrow + me) * pieces
    sk_pad[...] = jnp.zeros_like(sk_pad)
    sk_pad[:sk, :] = sketch[...]
    sk_hot = jnp.where(both_col == spots, 1.0, 0.0).astype(bf16)
    k_high, k_mid, k_low = three(sk_pad[...])
    sk_pick[...] = (dot(sk_hot, k_low, NT) + dot(sk_hot, k_mid, NT)) + dot(sk_hot, k_high, NT)

    def slots_of(owner):
        return pl.ds(pl.multiple_of(owner * slots, slots), slots)

    def sk_reduce(d):
        return remote(sk_pick.at[slots_of(lax.rem(me + d, nrow)), :], sk_in.at[d], ks_s.at[d], ks_r.at[d], beside(d))

    def sk_along(d):
        return remote(sk_part.at[0], sk_part.at[d], kz_s.at[d], kz_r.at[d], along(d))

    offset = z * columns
    local = pivots[...] - offset
    mine = (local >= 0) & (local < columns)
    before = local < 0

    pl.semaphore_wait(barrier, nrow + ncol - 2)

    @pl.loop(1, nrow)
    def _(d):
        sk_reduce(d).start()

    former_hot = jnp.where(iota((n, n), 0) == partner, 1.0, 0.0).astype(bf16)
    size = rows // chunks

    picked[...] = jnp.zeros_like(picked)

    @pl.loop(0, tiles)
    def _(t):
        at = pl.multiple_of(t * n, n)
        onehot = jnp.where(iota((n, n), 0) + at == local, 1.0, 0.0).astype(bf16)
        picked[...] += pick3(three(x[:, pl.ds(at, n)]), onehot)

    @pl.when(z == 0)
    def _():
        moved_in[...] = pick3(three(x[:, :n]), former_hot)

    def right(c):
        at = pl.ds(pl.multiple_of(c * size, size), size)
        return remote(to_right.at[at, :], from_left.at[at, :], zr_s.at[c], zr_r.at[c], {"col": z + 1})

    def left(c):
        at = pl.ds(pl.multiple_of(c * size, size), size)
        return remote(to_left.at[at, :], from_right.at[at, :], zl_s.at[c], zl_r.at[c], {"col": z - 1})

    @pl.loop(0, chunks + skew * (ncol - 1))
    def _(t):
        c = t - skew * z

        @pl.when((c >= 0) & (c < chunks))
        def _():
            at = pl.ds(pl.multiple_of(c * size, size), size)

            @pl.when(z > 0)
            def _():
                right(c).wait_recv()
                moved_in[at, :] = from_left[at, :]

            @pl.when(z < ncol - 1)
            def _():
                to_right[at, :] = jnp.where(mine, picked[at, :], moved_in[at, :])
                right(c).start()

        e = t - skew * (ncol - 1 - z)

        @pl.when((e >= 0) & (e < chunks))
        def _():
            at = pl.ds(pl.multiple_of(e * size, size), size)

            @pl.when(z < ncol - 1)
            def _():
                left(e).wait_recv()
                panel[at, :] = jnp.where(mine, picked[at, :], from_right[at, :])

            @pl.when(z == ncol - 1)
            def _():
                panel[at, :] = picked[at, :]

            @pl.when(z > 0)
            def _():
                to_left[at, :] = panel[at, :]
                left(e).start()

    panel[...] = jnp.where(before, moved_in[...], panel[...])

    half = n // 2
    columns_of = panel[...].T
    gram[...] = dot(columns_of, panel[...], precision=highest)
    first = remote(gram, gram_in, g1.at[0], g1.at[1], {"row": mate})
    first.start()

    left_parts = two(columns_of)
    former = three(moved_in[...])
    wanted = piv_col - offset
    usable = piv_col >= n

    first.wait()
    mine_rows = pl.ds(pl.multiple_of(core * half, half), half)
    other_rows = pl.ds(pl.multiple_of((1 - core) * half, half), half)
    quarter = half // ncol

    def gram_rows(place):
        return pl.ds(pl.multiple_of(core * half + place * quarter, quarter), quarter)

    gram_parts[0, :, :] = gram[gram_rows(z), :] + gram_in[gram_rows(z), :]
    aug[:, n:] = jnp.where(iota((n, n), 0) == iota((n, n), 1), 1.0, 0.0).astype(f32)

    def gram_to(d):
        return remote(gram_parts.at[0], gram_parts.at[d], g2_s.at[d], g2_r.at[d], {"row": peer(d)})

    for d in range(1, chips):
        gram_to(d).start()

    def gram_along(d, place):
        at = gram_rows(place)
        return remote(aug.at[at, :n], aug.at[at, :n], gz_s.at[d], gz_r.at[d], along(d))

    last = remote(aug.at[mine_rows, :n], aug.at[mine_rows, :n], g3.at[0], g3.at[1], {"row": mate})

    def gram_over_chips():
        for d in range(1, chips):
            gram_to(d).wait()
        total = jnp.zeros((quarter, n), f32)
        for d in range(chips):
            total = total + gram_parts[lax.rem(chip + chips - d, chips), :, :]
        aug[gram_rows(z), :n] = total
        for d in range(1, ncol):
            gram_along(d, z).start()

    def gram_over_line():
        for d in range(1, ncol):
            gram_along(d, z).wait_send()
            gram_along(d, lax.rem(z + ncol - d, ncol)).wait_recv()
        last.start()

    def out_copy(t):
        at = pl.ds(pl.multiple_of(t * n, n), n)
        return pltpu.make_async_copy(perm.at[:, at], perm_hbm.at[:, at], out_sem.at[t])

    def part(owner):
        return pl.ds(pl.multiple_of(owner * share, share), share)

    def to_mate(c):
        return remote(product.at[part(2 * c + 1 - core), :], core_in.at[c], c_s.at[c], c_r.at[c], {"row": mate})

    def reduce_to(d):
        return remote(totals.at[lax.rem(chip + d, chips)], reduce_in.at[d], r_s.at[d], r_r.at[d], {"row": peer(d)})

    def add_cores(c):
        to_mate(c).wait()
        totals[c, :, :] = product[part(2 * c + core), :] + core_in[c, :, :]

    def send_sums(d):
        add_cores(lax.rem(chip + d, chips))
        reduce_to(d).start()

    per_tile = n // share
    per_chip = 2 * share // n
    begin = lax.rem(chip + 1, chips) * 2 * share // n

    @pl.loop(0, tiles)
    def _(u):
        t = lax.rem(begin + u, tiles)
        at = pl.multiple_of(t * n, n)
        place = (iota((n, n), 1) + at == wanted) & usable
        place = jnp.where(place, 1.0, 0.0)
        keep = 1.0 - jnp.sum(place, axis=0, keepdims=True)
        tile = x[:, pl.ds(at, n)] * keep + pick3(former, place.astype(bf16))
        tile = jnp.where((z == 0) & (t == 0), panel[...], tile)
        perm[:, pl.ds(at, n)] = tile
        out_copy(t).start()
        product[pl.ds(at, n), :] = dot3(left_parts, two(tile)).T

        for i in range(per_tile):
            owner = t * per_tile + i

            @pl.when(lax.rem(owner, 2) != core)
            def _():
                to_mate(owner // 2).start()

        if per_chip > 0:
            ready = (u + 1) // per_chip

            @pl.when((lax.rem(u + 1, per_chip) == 0) & (ready >= 2))
            def _():
                send_sums(ready - 1)

        @pl.when(u == tiles // 2)
        def _():
            gram_over_chips()

        @pl.when(u == tiles - 1)
        def _():
            gram_over_line()

    if per_chip == 0:
        for d in range(1, chips):
            send_sums(d)
    add_cores(chip)

    @pl.loop(1, nrow)
    def _(d):
        sk_reduce(d).wait()

    sk_part[0, :, :] = sk_pick[slots_of(me), :] + jnp.sum(sk_in[1:, :, :], axis=0)
    for d in range(1, ncol):
        sk_along(d).start()

    last.wait_send()
    remote(aug.at[other_rows, :n], aug.at[other_rows, :n], g3.at[0], g3.at[1], {"row": mate}).wait_recv()

    def gather_to(d):
        return remote(summed.at[part(me), :], summed.at[part(me), :], a_s.at[d], a_r.at[d], {"row": peer(d)})

    def gathered(d):
        at = part(origin(d) * 2 + core)
        return remote(summed.at[at, :], summed.at[at, :], a_s.at[d], a_r.at[d], {"row": peer(d)})

    def forward(d):
        at = part(origin(d) * 2 + core)
        return remote(summed.at[at, :], summed.at[at, :], f_s.at[d], f_r.at[d], {"row": mate})

    def forwarded(d):
        at = part(origin(d) * 2 + 1 - core)
        return remote(summed.at[at, :], summed.at[at, :], f_s.at[d], f_r.at[d], {"row": mate})

    def sk_gather_to(d):
        at = slots_of(me)
        return remote(sk_all.at[at, :], sk_all.at[at, :], ka_s.at[d], ka_r.at[d], {"row": peer(d)})

    def sk_gathered(d):
        at = slots_of(origin(d) * 2 + core)
        return remote(sk_all.at[at, :], sk_all.at[at, :], ka_s.at[d], ka_r.at[d], {"row": peer(d)})

    def sk_forward(d):
        at = slots_of(origin(d) * 2 + core)
        return remote(sk_all.at[at, :], sk_all.at[at, :], kf_s.at[d], kf_r.at[d], {"row": mate})

    def sk_forwarded(d):
        at = slots_of(origin(d) * 2 + 1 - core)
        return remote(sk_all.at[at, :], sk_all.at[at, :], kf_s.at[d], kf_r.at[d], {"row": mate})

    def finish_reduce():
        total = totals[chip, :, :]
        for d in range(1, chips):
            reduce_to(d).wait()
            total = total + reduce_in[d, :, :]
        summed[part(me), :] = total
        for d in range(1, chips):
            gather_to(d).start()
        forward(0).start()
        for d in range(1, ncol):
            sk_along(d).wait()
        sk_all[slots_of(me), :] = jnp.sum(sk_part[...], axis=0)
        for d in range(1, chips):
            sk_gather_to(d).start()
        sk_forward(0).start()

    def finish_gather():
        for d in range(1, chips):
            gathered(d).wait_recv()
            forward(d).start()

    blocks = n // width
    for b in range(blocks):
        cholesky_block(aug, linv, b, width)
        if b == blocks // 2 - 1:
            finish_reduce()
    finish_gather()
    for d in range(1, chips):
        sk_gathered(d).wait_recv()
        sk_forward(d).start()

    inverse = dot3(two(linv[...]), two(linv[...]), TN)
    w_high[...], w_low[...] = two(dot3(two(panel[...]), two(inverse)))
    own = two(summed[part(me), :])
    upper_out[...] = dot3(two(linv[...]), own, NT)
    solved = dot3(two(inverse), own, NT)

    for d in range(chips):
        forwarded(d).wait_recv()

    @pl.loop(0, tiles)
    def _(t):
        at = pl.ds(pl.multiple_of(t * n, n), n)
        high, low = two(summed[at, :].T)
        s_high[:, at] = high
        s_low[:, at] = low

    for d in range(chips):
        sk_forwarded(d).wait_recv()
    into = jnp.where((spots == piv_col) & (piv_col >= n), 1.0, 0.0)
    leading = jnp.where(spots == iota((n, 1), 0), 1.0, 0.0)
    chosen = jnp.concatenate([leading, into], axis=0)
    stay = 1.0 - jnp.sum(chosen, axis=0, keepdims=True)
    turned_all = sk_all[...].T
    changed = pick3(three(turned_all), chosen.astype(bf16)) - dot3(two(turned_all[:, :n]), two(solved))
    sketch_out[...] = sketch[...] * stay + changed[:sk, :]

    for d in range(1, chips):
        gather_to(d).wait_send()
        sk_gather_to(d).wait_send()
    for d in range(chips):
        forward(d).wait_send()
        sk_forward(d).wait_send()

    @pl.loop(0, chunks)
    def _(c):
        @pl.when(z < ncol - 1)
        def _():
            right(c).wait_send()

        @pl.when(z > 0)
        def _():
            left(c).wait_send()

    @pl.loop(0, tiles)
    def _(t):
        out_copy(t).wait()


def project(perm, w_high, w_low, s_high, s_low, upper, sketch, out, upper_out, sketch_out):
    @pl.when(pl.program_id(0) == 0)
    def _():
        upper_out[...] = upper[...]
        sketch_out[...] = sketch[...]

    out[...] = perm[...] - dot3((w_high[...], w_low[...]), (s_high[...], s_low[...]))


def per_device(nrow, ncol, matrix, pivots, sketch):
    rows, columns = matrix.shape
    n = pivots.shape[0]
    sk, pieces = sketch.shape
    padded = (sk + 127) // 128 * 128
    chunks = 20
    skew = 3
    width = 64
    chips = nrow // 2
    share = columns // nrow
    slots = 2 * n // nrow
    vmem = pl.BlockSpec(memory_space=pltpu.VMEM)
    full = pltpu.VMEM((rows, n), f32)
    dma = pltpu.SemaphoreType.DMA
    shape = jax.ShapeDtypeStruct
    perm, w_high, w_low, s_high, s_low, upper, new_sketch = pl.pallas_call(
        functools.partial(kernel, nrow, ncol, chunks, skew, width),
        out_shape=[
            shape((rows, columns), f32),
            shape((rows, n), bf16),
            shape((rows, n), bf16),
            shape((n, columns), bf16),
            shape((n, columns), bf16),
            shape((n, share), f32),
            shape((sk, pieces), f32),
        ],
        in_specs=[vmem] * 3,
        out_specs=[pl.BlockSpec(memory_space=pl.ANY)] + [vmem] * 6,
        scratch_shapes=[
            full, full, full, full, full, full, full,
            pltpu.VMEM((rows, columns), f32),
            pltpu.VMEM((columns, n), f32),
            pltpu.VMEM((columns, n), f32),
            pltpu.VMEM((chips, share, n), f32),
            pltpu.VMEM((chips, share, n), f32),
            pltpu.VMEM((chips, share, n), f32),
            pltpu.VMEM((n, n), f32),
            pltpu.VMEM((n, n), f32),
            pltpu.VMEM((chips, n // 2 // ncol, n), f32),
            pltpu.VMEM((n, 2 * n), f32),
            pltpu.VMEM((n, n), f32),
            pltpu.VMEM((padded, pieces), f32),
            pltpu.VMEM((2 * n, padded), f32),
            pltpu.VMEM((nrow, slots, padded), f32),
            pltpu.VMEM((ncol, slots, padded), f32),
            pltpu.VMEM((2 * n, padded), f32),
            dma((chunks,)), dma((chunks,)), dma((chunks,)), dma((chunks,)),
            dma((2,)), dma((chips,)), dma((chips,)), dma((2,)),
            dma((chips,)), dma((chips,)), dma((chips,)), dma((chips,)),
            dma((chips,)), dma((chips,)), dma((chips,)), dma((chips,)),
            dma((columns // n,)),
            dma((ncol,)), dma((ncol,)),
            dma((nrow,)), dma((nrow,)), dma((ncol,)), dma((ncol,)),
            dma((chips,)), dma((chips,)), dma((chips,)), dma((chips,)),
        ],
        compiler_params=pltpu.CompilerParams(
            collective_id=0, has_side_effects=True, vmem_limit_bytes=56 * 1024 * 1024
        ),
        cost_estimate=pl.CostEstimate(
            flops=20 * rows * n * columns, bytes_accessed=8 * rows * columns, transcendentals=0
        ),
    )(matrix, pivots[None, :], sketch)

    tile = 2 * n
    whole = pl.BlockSpec((rows, n), lambda i: (0, 0))
    across = pl.BlockSpec((n, tile), lambda i: (0, i))
    small = [pl.BlockSpec(a.shape, lambda i: (0, 0)) for a in (upper, new_sketch)]
    trailing, upper, new_sketch = pl.pallas_call(
        project,
        grid=(columns // tile,),
        out_shape=[shape((rows, columns), f32), shape(upper.shape, f32), shape(new_sketch.shape, f32)],
        in_specs=[pl.BlockSpec((rows, tile), lambda i: (0, i)), whole, whole, across, across]
        + small,
        out_specs=[pl.BlockSpec((rows, tile), lambda i: (0, i))] + small,
        compiler_params=pltpu.CompilerParams(vmem_limit_bytes=56 * 1024 * 1024),
    )(perm, w_high, w_low, s_high, s_low, upper, new_sketch)
    return (upper, trailing, new_sketch)


def solution(mesh):
    return jax.shard_map(
        functools.partial(per_device, mesh.shape["row"], mesh.shape["col"]),
        mesh=mesh,
        in_specs=(P("row", "col"), P(), P(None, ("col", "row"))),
        out_specs=(P(None, ("col", "row")), P("row", "col"), P(None, ("col", "row"))),
        check_vma=False,
    )
```
